128 devices in a mesh: fsdp: 16 (over x_lo, z, core), tp: 8 (over x_hi, y).
Axes of the slice: x: 4 (x_hi: 2, x_lo: 2; x = x_hi * 2 + x_lo), y: 4, z: 4, core: 2. Of those that a mesh axis runs over, the one named last changes fastest.
Arguments:
- weight_master: float32 [4096, 18560], P(('fsdp', 'tp')), may hold values from -0.09375 to 0.09375
- weight_grad: bfloat16 [4096, 18560], P(('fsdp', 'tp')), may hold values from -6 to 6
- weight_first: float32 [4096, 18560], P(('fsdp', 'tp')), may hold values from -2 to 2
- weight_second: float32 [4096, 18560], P(('fsdp', 'tp')), may hold values from 0.05 to 0.5
- conv_master: float32 [5, 10240], P(None, ('fsdp', 'tp')), may hold values from -3 to 3
- conv_grad: bfloat16 [5, 10240], P(None, ('fsdp', 'tp')), may hold values from -6 to 6
- conv_first: float32 [5, 10240], P(None, ('fsdp', 'tp')), may hold values from -2 to 2
- conv_second: float32 [5, 10240], P(None, ('fsdp', 'tp')), may hold values from 0.05 to 0.5
- learn_rate: float32 [1], replicated, may hold values from 0.005 to 0.02
- segment_offsets: int32 [5], replicated, may hold values from 0 to 18432, as said below
- head_order: int32 [128], replicated, may hold values from 0 to 127, each once
- group_order: int32 [8], replicated, may hold values from 0 to 7, each once
- hidden_input: bfloat16 [3, 768, 4096], P(None, 'fsdp'), may hold values from -6 to 6
- scan_state: bfloat16 [768, 128, 64, 128], P('fsdp', 'tp'), may hold values from -6 to 6
- conv_heads: bfloat16 [768, 3, 8192], P('fsdp', None, 'tp'), may hold values from -6 to 6
- conv_groups: bfloat16 [768, 3, 2, 8, 128], P('fsdp', None, None, 'tp'), may hold values from -6 to 6
- decay_log: float32 [128], replicated, may hold values from 0 to 2.5
- delta_bias: float32 [128], replicated, may hold values from -3 to 0
- skip_gain: float32 [128], replicated, may hold values from 0.5 to 1.5
- norm_gain: float32 [8192], replicated, may hold values from 0.5 to 1.5
Outputs:
- mixer_out: bfloat16 [3, 768, 8192], P(None, 'fsdp', 'tp')
The draws below stay inside these ranges and needn't reach their ends.
Inputs may be any that keep to these rules, and one draw needn't show every extreme that they name: `segment_offsets`: the five segments z, x, B, C, dt have lengths 8192, 8192, 1024, 1024, 128 and together cover columns 0 to 18559 without gaps; dt is the last segment, the order of the other four varies. `head_order`: each head once; owner i of tp holds head slots i * 128 / 8 onward. `group_order`: each group once; owner i of tp holds group slots i * 8 / 8 onward.
All inputs are finite; a program needn't handle non-finite values.
Results may differ from the reference program's by a relative error of at most 0.002.
The reference program's roundings to bfloat16 on the way (of `new_weight`, `new_conv` and `projected`) count: a program that leaves them out, or rounds other values in their place, can miss the bound.
Values may be sent and summed in bfloat16 or wider, within the bound.
No kernel may reach another device: no remote copies, remote signals or barrier semaphores. Data moves between devices by JAX's collectives and lax.ppermute only.
A program may use at most 256 MiB of HBM per device.

```python
import math
import jax
import jax.numpy as jnp
from jax import lax

D = 4096
HEADS = 128
HEAD_DIM = 64
GROUPS = 8
STATE = 128
TAPS = 4
STEPS = 3
ADAM_STEP = 100
ROWS = 48
REQUESTS = 768
INNER = 8192
JOINED = 18560
CONV_WIDTH = 10240


def draw_segment_offsets(key, part):
    key = jax.random.fold_in(key, 11)
    front = jax.random.permutation(key, 4)
    order = jnp.concatenate([front, jnp.array([4], dtype=jnp.int32)]).astype(jnp.int32)
    lengths = jnp.array([HEADS * HEAD_DIM, HEADS * HEAD_DIM, GROUPS * STATE, GROUPS * STATE, HEADS], dtype=jnp.int32)
    ordered = lengths[order]
    starts = (jnp.cumsum(ordered) - ordered).astype(jnp.int32)
    return jnp.zeros((5,), jnp.int32).at[order].set(starts)


def steps_of(own_key, extent, cuts, least, top_value):
    def one(dim, shards_of):
        heights = jax.random.uniform(jax.random.fold_in(jax.random.fold_in(own_key, 6), dim), (shards_of,), jnp.float32, least / len(cuts), top_value / len(cuts))
        return jnp.repeat(jnp.exp(heights), extent[dim] // shards_of).reshape((-1,) + (1,) * (len(extent) - dim - 1))

    factor_of = one(*cuts[0])
    for cut in cuts[1:]:
        factor_of = factor_of * one(*cut)
    return factor_of


def noise(own_key, shape, deviation, limit, cuts=(), kind=jnp.bfloat16):
    loudness = steps_of(own_key, shape, cuts, -0.22, 0.18) if cuts else 1.0
    result = jax.random.normal(own_key, shape, jnp.float32) * deviation * loudness
    return jnp.minimum(jnp.maximum(result, -limit), limit).astype(kind)


def setup_inputs(seed: int = 0) -> dict:
    seeds = jax.random.split(jax.random.key(seed), 21)
    weight_master = noise(seeds[0], (D, JOINED), D ** -0.5, 0.09375, ((0, 128),), jnp.float32)
    weight_grad = noise(seeds[1], (D, JOINED), 1.0, 6.0, ((0, 128),))
    weight_first = noise(seeds[2], (D, JOINED), 0.3, 2.0, ((0, 128),), jnp.float32)
    weight_second = jnp.clip(jnp.exp(math.log(0.5) - 2.3025851 * jax.random.uniform(seeds[3], (D, JOINED), jnp.float32) ** steps_of(seeds[3], (D, JOINED), ((0, 128),), -0.2, 0.2)), 0.05, 0.5)
    conv_master = noise(seeds[4], (TAPS + 1, CONV_WIDTH), 0.5, 3.0, ((1, 128),), jnp.float32)
    conv_grad = noise(seeds[5], (TAPS + 1, CONV_WIDTH), 1.0, 6.0, ((1, 128),))
    conv_first = noise(seeds[6], (TAPS + 1, CONV_WIDTH), 0.3, 2.0, ((1, 128),), jnp.float32)
    conv_second = jnp.clip(jnp.exp(math.log(0.5) - 2.3025851 * jax.random.uniform(seeds[7], (TAPS + 1, CONV_WIDTH), jnp.float32) ** steps_of(seeds[7], (TAPS + 1, CONV_WIDTH), ((1, 128),), -0.2, 0.2)), 0.05, 0.5)
    learn_rate = jnp.clip(jnp.exp(jax.random.uniform(seeds[8], (1,), jnp.float32, math.log(0.005), math.log(0.02))), 0.005, 0.02)
    segment_offsets = draw_segment_offsets(jax.random.fold_in(seeds[20], 71), 0)
    head_order = jax.random.permutation(seeds[10], HEADS).astype(jnp.int32)
    group_order = jax.random.permutation(seeds[11], GROUPS).astype(jnp.int32)
    hidden_input = noise(seeds[12], (STEPS, REQUESTS, D), 1.0, 6.0, ((1, 16),))
    scan_state = noise(seeds[13], (REQUESTS, HEADS, HEAD_DIM, STATE), 1.0, 6.0, ((0, 16), (1, 8)))
    conv_heads = noise(seeds[14], (REQUESTS, TAPS - 1, INNER), 1.0, 6.0, ((0, 16), (2, 8)))
    conv_groups = noise(seeds[15], (REQUESTS, TAPS - 1, 2, GROUPS, STATE), 1.0, 6.0, ((0, 16), (3, 8)))
    decay_log = jnp.clip(jax.random.uniform(seeds[16], (HEADS,), jnp.float32, 0.0, 2.5), 0.0, 2.5)
    delta_bias = jnp.clip(jax.random.uniform(seeds[17], (HEADS,), jnp.float32, -3.0, 0.0), -3.0, 0.0)
    skip_gain = jnp.clip(jax.random.uniform(seeds[18], (HEADS,), jnp.float32, 0.5, 1.5), 0.5, 1.5)
    norm_gain = jnp.clip(1.0 + 0.1 * jax.random.normal(seeds[19], (INNER,), jnp.float32), 0.5, 1.5)
    return dict(weight_master=weight_master, weight_grad=weight_grad, weight_first=weight_first, weight_second=weight_second, conv_master=conv_master, conv_grad=conv_grad, conv_first=conv_first, conv_second=conv_second, learn_rate=learn_rate, segment_offsets=segment_offsets, head_order=head_order, group_order=group_order, hidden_input=hidden_input, scan_state=scan_state, conv_heads=conv_heads, conv_groups=conv_groups, decay_log=decay_log, delta_bias=delta_bias, skip_gain=skip_gain, norm_gain=norm_gain)


beta_one = 0.9
beta_two = 0.95
adam_eps = 1e-08
weight_decay = 0.1
norm_eps = 1e-05

def adamw(master, gradient, first, second, rate):
    slope = gradient.astype(jnp.float32)
    moment_one = beta_one * first + (1.0 - beta_one) * slope
    moment_two = beta_two * second + (1.0 - beta_two) * slope * slope
    fixed_one = moment_one / (1.0 - beta_one ** ADAM_STEP)
    fixed_two = moment_two / (1.0 - beta_two ** ADAM_STEP)
    update = fixed_one / (jnp.sqrt(fixed_two) + adam_eps) + weight_decay * master
    return (master - rate * update).astype(jnp.bfloat16)

def conv_silu(values, stored, taps):
    window = jnp.concatenate([stored.astype(jnp.float32), jnp.swapaxes(values, 0, 1).astype(jnp.float32)], axis=1)
    weights = taps.astype(jnp.float32)
    outputs = []
    for moment in range(values.shape[0]):
        total = weights[TAPS]
        for lag in range(TAPS):
            total = total + weights[lag] * window[:, moment + lag]
        outputs.append(jax.nn.silu(total))
    return jnp.stack(outputs).astype(jnp.bfloat16)

def scan_heads(state_in, x_heads, b_heads, c_heads, delta_raw, decay_rate, bias, skip):
    state = state_in.astype(jnp.float32)
    outputs = []
    for moment in range(x_heads.shape[0]):
        delta = jax.nn.softplus(delta_raw[moment].astype(jnp.float32) + bias)
        keep = jnp.exp(delta * decay_rate)
        values = x_heads[moment]
        state = state * keep[:, :, None, None] + (delta[:, :, None] * values)[:, :, :, None] * b_heads[moment][:, :, None, :]
        read = jnp.einsum('rhpn,rhn->rhp', state, c_heads[moment], precision=lax.Precision.HIGHEST)
        outputs.append(read + skip[None, :, None] * values)
    return jnp.stack(outputs)

def reference(weight_master, weight_grad, weight_first, weight_second, conv_master, conv_grad, conv_first, conv_second, learn_rate, segment_offsets, head_order, group_order, hidden_input, scan_state, conv_heads, conv_groups, decay_log, delta_bias, skip_gain, norm_gain):
    rate = learn_rate[0]
    new_weight = adamw(weight_master, weight_grad, weight_first, weight_second, rate)
    new_conv = adamw(conv_master, conv_grad, conv_first, conv_second, rate)
    inner = HEADS * HEAD_DIM
    width_groups = GROUPS * STATE
    flat = hidden_input.reshape(STEPS * REQUESTS, D)
    projected = jnp.dot(flat, new_weight, preferred_element_type=jnp.float32).astype(jnp.bfloat16)
    projected = projected.reshape(STEPS, REQUESTS, JOINED)
    lanes = jnp.arange(HEAD_DIM, dtype=jnp.int32)
    state_lanes = jnp.arange(STATE, dtype=jnp.int32)
    head_cols = (head_order[:, None] * HEAD_DIM + lanes[None, :]).reshape(-1).astype(jnp.int32)
    group_cols = (group_order[:, None] * STATE + state_lanes[None, :]).reshape(-1).astype(jnp.int32)
    gate_in = jnp.take(projected, segment_offsets[0] + head_cols, axis=2)
    x_in = jnp.take(projected, segment_offsets[1] + head_cols, axis=2)
    b_in = jnp.take(projected, segment_offsets[2] + group_cols, axis=2)
    c_in = jnp.take(projected, segment_offsets[3] + group_cols, axis=2)
    delta_raw = jnp.take(projected, segment_offsets[4] + head_order, axis=2)
    x_conv = conv_silu(x_in, conv_heads, jnp.take(new_conv, head_cols, axis=1))
    group_taps = jnp.take(new_conv, jnp.concatenate([inner + group_cols, inner + width_groups + group_cols]), axis=1)
    group_conv = conv_silu(jnp.concatenate([b_in, c_in], axis=2), conv_groups.reshape(REQUESTS, TAPS - 1, 2 * width_groups), group_taps)
    group_conv = group_conv.reshape(STEPS, REQUESTS, 2, GROUPS, STATE).astype(jnp.float32)
    per_group = HEADS // GROUPS
    head_group = head_order // per_group
    pick = (group_order[None, :] == head_group[:, None]).astype(jnp.float32)
    b_heads = jnp.einsum('srqn,hq->srhn', group_conv[:, :, 0], pick, precision=lax.Precision.HIGHEST)
    c_heads = jnp.einsum('srqn,hq->srhn', group_conv[:, :, 1], pick, precision=lax.Precision.HIGHEST)
    x_heads = x_conv.astype(jnp.float32).reshape(STEPS, REQUESTS, HEADS, HEAD_DIM)
    decay_rate = -jnp.exp(decay_log[head_order])
    bias = delta_bias[head_order]
    skip = skip_gain[head_order]
    blocks = REQUESTS // ROWS

    def by_block(array):
        shaped = array.reshape((array.shape[0], blocks, ROWS) + array.shape[2:])
        return jnp.swapaxes(shaped, 0, 1)

    def one_block(pieces):
        return scan_heads(pieces[0], pieces[1], pieces[2], pieces[3], pieces[4], decay_rate, bias, skip)
    scanned = lax.map(one_block, (scan_state.reshape(blocks, ROWS, HEADS, HEAD_DIM, STATE), by_block(x_heads), by_block(b_heads), by_block(c_heads), by_block(delta_raw)))
    scanned = jnp.swapaxes(scanned, 0, 1).reshape(STEPS, REQUESTS, HEADS, HEAD_DIM)
    gated = scanned * jax.nn.silu(gate_in.astype(jnp.float32).reshape(STEPS, REQUESTS, HEADS, HEAD_DIM))
    member = (head_group[:, None] == jnp.arange(GROUPS, dtype=jnp.int32)[None, :]).astype(jnp.float32)
    squares = jnp.einsum('srh,hg->srg', lax.optimization_barrier(jnp.sum(gated * gated, axis=3)), member, precision=lax.Precision.HIGHEST)
    scale = lax.rsqrt(squares / (per_group * HEAD_DIM) + norm_eps)
    scale_heads = jnp.einsum('srg,hg->srh', scale, member, precision=lax.Precision.HIGHEST)
    gain_slots = norm_gain[head_cols].reshape(HEADS, HEAD_DIM)
    mixer_out = gated * scale_heads[:, :, :, None] * gain_slots[None, None]
    return mixer_out.astype(jnp.bfloat16).reshape(STEPS, REQUESTS, inner)
```

```python
import functools

import jax
import jax.numpy as jnp
from jax import lax
from jax.experimental import pallas as pl
from jax.experimental.pallas import tpu as pltpu
from jax.sharding import PartitionSpec as P

TAPS = 4
ADAM_STEP = 100
STEPS = 3
ROWS = 48
FLAT = STEPS * ROWS
HEADS = 128
GROUPS = 8
HEAD_DIM = 64
STATE = 128
OWN_HEADS = 16
SPAN = OWN_HEADS * HEAD_DIM
JOINED = 18560
PIECE = 3712
SHARD = 80
INNER = HEADS * HEAD_DIM
FIRST = 3 * 128 + SPAN

beta_one = 0.9
beta_two = 0.95
adam_eps = 1e-08
weight_decay = 0.1
norm_eps = 1e-05
HIGH = lax.Precision.HIGHEST


def adamw(master, gradient, first, second, rate):
    slope = gradient.astype(jnp.float32)
    moment_one = beta_one * first + (1.0 - beta_one) * slope
    moment_two = beta_two * second + (1.0 - beta_two) * slope * slope
    fixed_one = moment_one / (1.0 - beta_one**ADAM_STEP)
    fixed_two = moment_two / (1.0 - beta_two**ADAM_STEP)
    update = fixed_one / (jnp.sqrt(fixed_two) + adam_eps) + weight_decay * master
    return (master - rate * update).astype(jnp.bfloat16)


def refit_kernel(rate, offsets, heads, groups, order, master, grad, first, second, conv, front, gate, work):
    step = pl.program_id(0)
    for j in range(PIECE // 128):
        cols = slice(j * 128, (j + 1) * 128)
        new = adamw(master[:, cols], grad[:, cols], first[:, cols], second[:, cols], rate[0])
        work[:, pl.ds(pl.multiple_of(step * PIECE + j * 128, 128), 128)] = new.astype(jnp.float32)

    @pl.when(step == JOINED // PIECE - 1)
    def _():
        lane = lax.broadcasted_iota(jnp.int32, (32, 128), 1)
        dt = work[:, pl.ds(pl.multiple_of(offsets[4], 128), 128)]
        onehot = (lax.broadcasted_iota(jnp.int32, (HEADS, HEADS), 0) == order[...]).astype(jnp.bfloat16)
        dt = jnp.dot(dt.astype(jnp.bfloat16), onehot, preferred_element_type=jnp.float32)

        def block(start):
            return work[:, pl.ds(pl.multiple_of(start, 128), 128)]

        def half(start, head, low):
            wide = block(start + (head // 2) * 128)
            turn = (head % 2) != (0 if low else 1)
            return jnp.where(turn, pltpu.roll(wide, 64, 1), wide)

        for owner in range(8):
            for k in range(8):
                low = heads[owner * OWN_HEADS + 2 * k]
                high = heads[owner * OWN_HEADS + 2 * k + 1]
                for segment, out, at in ((1, front, 384), (0, gate, 0)):
                    start = offsets[segment]
                    both = jnp.where(lane < 64, half(start, low, True), half(start, high, False))
                    out[owner, :, at + k * 128 : at + (k + 1) * 128] = both.astype(jnp.bfloat16)
            group = groups[owner]
            front[owner, :, 0:128] = block(offsets[2] + group * 128).astype(jnp.bfloat16)
            front[owner, :, 128:256] = block(offsets[3] + group * 128).astype(jnp.bfloat16)
            mine = dt if owner == 0 else pltpu.roll(dt, 128 - 16 * owner, 1)
            front[owner, :, 256:384] = jnp.where(lane < 16, mine, conv[...]).astype(jnp.bfloat16)


def refit(rate, offsets, heads, groups, master, grad, first, second, conv):
    smem = pl.BlockSpec(memory_space=pltpu.SMEM)
    piece = pl.BlockSpec((32, PIECE), lambda i: (0, i))
    whole = lambda shape: pl.BlockSpec(shape, lambda i: (0,) * len(shape))
    return pl.pallas_call(
        refit_kernel,
        grid=(JOINED // PIECE,),
        in_specs=[smem, smem, smem, smem, whole((1, HEADS)), piece, piece, piece, piece, whole((32, 128))],
        out_specs=[whole((8, 32, FIRST)), whole((8, 32, SPAN))],
        out_shape=[
            jax.ShapeDtypeStruct((8, 32, FIRST), jnp.bfloat16),
            jax.ShapeDtypeStruct((8, 32, SPAN), jnp.bfloat16),
        ],
        scratch_shapes=[pltpu.VMEM((32, JOINED), jnp.float32)],
        compiler_params=pltpu.CompilerParams(vmem_limit_bytes=40 * 2**20),
        name="refit",
    )(rate, offsets, heads, groups, heads.reshape(1, HEADS), master, grad, first, second, conv)


def silu(value):
    return value * jax.nn.sigmoid(value)


def convolve(inputs, stored, taps):
    window = [stored[j].astype(jnp.float32) for j in range(TAPS - 1)] + inputs
    outputs = []
    for moment in range(STEPS):
        total = taps[TAPS : TAPS + 1]
        for lag in range(TAPS):
            total = total + taps[lag : lag + 1] * window[moment + lag]
        outputs.append(silu(total).astype(jnp.bfloat16))
    return outputs


def rounded(ours, theirs, moment, cols=slice(None)):
    rows = slice(moment * ROWS, (moment + 1) * ROWS)
    return (ours[rows, cols] + theirs[rows, cols]).astype(jnp.bfloat16).astype(jnp.float32)


def groups_kernel(ours, theirs, stored, taps, out, dt):
    inputs = [rounded(ours, theirs, t, slice(0, 256)) for t in range(STEPS)]
    for t, value in enumerate(convolve(inputs, stored, taps[...])):
        out[t] = value
        dt[t] = rounded(ours, theirs, t, slice(256, 384)).astype(jnp.bfloat16)


def state_kernel(state, b_all, c_all, mask, out, pair):
    chosen = mask[...]
    for r in range(8):
        c = c_all[r]
        b = b_all[r]
        read = lax.dot_general(
            c.astype(jnp.bfloat16),
            state[r].reshape(SPAN, STATE),
            (((1,), (1,)), ((), ())),
            preferred_element_type=jnp.float32,
        )
        n = 0
        for t in range(STEPS):
            rows = slice(8 * t, 8 * t + 8)
            out[t, r : r + 1, :] = jnp.sum(read[rows] * chosen, axis=0, keepdims=True)
            for s in range(t + 1):
                both = jnp.sum(c[rows] * b[8 * s : 8 * s + 8], axis=1, keepdims=True)
                pair[n, r : r + 1, :] = jnp.sum(both * chosen, axis=0, keepdims=True)
                n += 1


def scan_kernel(ours, theirs, stored, taps, read, pair, dt, spread, params, out):
    inputs = [rounded(ours, theirs, t) for t in range(STEPS)]
    values = [v.astype(jnp.float32) for v in convolve(inputs, stored, taps[...])]
    rate = -jnp.exp(params[0:1])
    bias = params[1:2]
    skip = params[2:3]
    keeps, driven = [], []
    for t in range(STEPS):
        raw = jnp.dot(dt[t], spread[...], preferred_element_type=jnp.float32)
        delta = jax.nn.softplus(raw + bias)
        keeps.append(jnp.exp(delta * rate))
        driven.append(delta * values[t])
    n = 0
    for t in range(STEPS):
        total = skip * values[t]
        offset = n + t
        after = None
        for s in range(t, -1, -1):
            term = pair[offset] * driven[s]
            total = total + (term if after is None else after * term)
            after = keeps[s] if after is None else after * keeps[s]
            offset -= 1
        out[t] = total + after * read[t]
        n += t + 1


def gate_kernel(ours, theirs, scanned, member, gated, squares):
    for t in range(STEPS):
        value = scanned[t] * silu(rounded(ours, theirs, t))
        gated[t] = value
        squares[t] = lax.dot_general(
            member[...], value * value, (((1,), (1,)), ((), ())), precision=HIGH, preferred_element_type=jnp.float32
        )


def norm_kernel(gated, squares, member, gain, out):
    for t in range(STEPS):
        scale = lax.rsqrt(squares[t] / SPAN + norm_eps)
        lanes = lax.dot_general(
            scale, member[...], (((0,), (0,)), ((), ())), precision=HIGH, preferred_element_type=jnp.float32
        )
        out[t] = (gated[t] * lanes * gain[...]).astype(jnp.bfloat16)


def call(kernel, shapes, *args):
    vmem = pl.BlockSpec(memory_space=pltpu.VMEM)
    return pl.pallas_call(
        kernel,
        in_specs=[vmem] * len(args),
        out_specs=[vmem] * len(shapes),
        out_shape=[jax.ShapeDtypeStruct(s, d) for s, d in shapes],
        compiler_params=pltpu.CompilerParams(vmem_limit_bytes=40 * 2**20),
        name=kernel.__name__,
    )(*args)


def read_state(state, b_all, c_all, mask):
    return pl.pallas_call(
        state_kernel,
        grid=(ROWS // 8,),
        in_specs=[
            pl.BlockSpec((8, OWN_HEADS, HEAD_DIM, STATE), lambda i: (i, 0, 0, 0)),
            pl.BlockSpec((8, 24, STATE), lambda i: (i, 0, 0)),
            pl.BlockSpec((8, 24, STATE), lambda i: (i, 0, 0)),
            pl.BlockSpec((8, SPAN), lambda i: (0, 0)),
        ],
        out_specs=[
            pl.BlockSpec((3, 8, SPAN), lambda i: (0, i, 0)),
            pl.BlockSpec((6, 8, SPAN), lambda i: (0, i, 0)),
        ],
        out_shape=[
            jax.ShapeDtypeStruct((3, ROWS, SPAN), jnp.float32),
            jax.ShapeDtypeStruct((6, ROWS, SPAN), jnp.float32),
        ],
        compiler_params=pltpu.CompilerParams(vmem_limit_bytes=40 * 2**20),
        name="read_state",
    )(state, b_all, c_all, mask)


def per_device(
    weight_master,
    weight_grad,
    weight_first,
    weight_second,
    conv_master,
    conv_grad,
    conv_first,
    conv_second,
    learn_rate,
    segment_offsets,
    head_order,
    group_order,
    hidden_input,
    scan_state,
    conv_heads,
    conv_groups,
    decay_log,
    delta_bias,
    skip_gain,
    norm_gain,
):
    owner = lax.axis_index("tp")
    side = lax.axis_index("fsdp") // 8
    across = [(i, (i + 8) % 16) for i in range(16)]
    planes = [[8 * s + i for i in range(8)] for s in range(2)]
    swap = lambda value: lax.ppermute(value, "fsdp", across)

    flat = hidden_input.reshape(FLAT, -1)
    depth = flat.shape[1] // 2
    near = lax.dynamic_slice_in_dim(flat, side * depth, depth, 1)
    far = swap(lax.dynamic_slice_in_dim(flat, (1 - side) * depth, depth, 1))
    rows = jnp.concatenate([near, far], axis=0)

    new_conv = adamw(conv_master, conv_grad, conv_first, conv_second, learn_rate[0])
    conv_lanes = jnp.pad(new_conv.astype(jnp.float32), ((0, 27), (16, 32)))
    front, gate = refit(
        learn_rate, segment_offsets, head_order, group_order,
        weight_master, weight_grad, weight_first, weight_second, conv_lanes,
    )

    def owned(value):
        value = lax.all_to_all(value, "tp", split_axis=0, concat_axis=0, tiled=True)
        return value.reshape(256, value.shape[2])

    def gathered(value):
        return lax.all_gather(value, "fsdp", axis_index_groups=planes, axis=0, tiled=True)

    front = gathered(owned(front))
    gate = gathered(owned(gate))

    my_heads = lax.dynamic_slice_in_dim(head_order, owner * OWN_HEADS, OWN_HEADS)
    pick_heads = my_heads[:, None] == jnp.arange(HEADS, dtype=jnp.int32)[None, :]
    lane_group = jnp.repeat(my_heads // OWN_HEADS, HEAD_DIM)
    member = (jnp.arange(GROUPS, dtype=jnp.int32)[:, None] == lane_group[None, :]).astype(jnp.float32)
    partner = owner ^ jnp.arange(GROUPS, dtype=jnp.int32)
    mask = (jnp.take(group_order, partner)[:, None] == lane_group[None, :]).astype(jnp.float32)
    spread = (jnp.arange(128, dtype=jnp.int32)[:, None] == (jnp.arange(SPAN, dtype=jnp.int32) // HEAD_DIM)[None, :])
    spread = spread.astype(jnp.bfloat16)
    params = jnp.stack([decay_log[my_heads], delta_bias[my_heads], skip_gain[my_heads]])
    params = jnp.repeat(params, HEAD_DIM, axis=1)
    gain = jnp.dot(
        pick_heads.astype(jnp.float32), norm_gain.reshape(HEADS, HEAD_DIM), precision=HIGH
    ).reshape(1, SPAN)
    stored_heads = jnp.swapaxes(conv_heads, 0, 1)
    stored_groups = jnp.swapaxes(conv_groups.reshape(ROWS, TAPS - 1, 2 * STATE), 0, 1)

    here = front.reshape(64, 32, FIRST)[:, :16, 256:384]
    there = swap(here)
    low = jnp.where(side == 0, here, there)
    high = jnp.where(side == 0, there, here)
    conv_all = jnp.concatenate([low, high], axis=0)[:, :5, 16 : 16 + SHARD]
    conv_all = jnp.swapaxes(conv_all, 0, 1).reshape(5, 128 * SHARD)
    head_taps = jnp.einsum(
        "hk,jkp->jhp",
        pick_heads.astype(jnp.bfloat16),
        conv_all[:, :INNER].reshape(5, HEADS, HEAD_DIM),
        preferred_element_type=jnp.float32,
    ).reshape(5, SPAN)
    my_group = lax.dynamic_slice_in_dim(group_order, owner, 1)
    pick_group = (my_group == jnp.arange(GROUPS, dtype=jnp.int32)).astype(jnp.bfloat16)
    group_taps = jnp.einsum(
        "g,jagn->jan",
        pick_group,
        conv_all[:, INNER:].reshape(5, 2, GROUPS, STATE),
        preferred_element_type=jnp.float32,
    ).reshape(5, 2 * STATE)

    product = lambda weights: jnp.dot(rows, weights, preferred_element_type=jnp.float32)
    first = product(front[:, :384])
    b_and_c, dt = call(
        groups_kernel,
        [((STEPS, ROWS, 2 * STATE), jnp.bfloat16), ((STEPS, ROWS, 128), jnp.bfloat16)],
        first[:FLAT], swap(first[FLAT:]), stored_groups, group_taps,
    )
    every = [b_and_c] + [
        lax.ppermute(b_and_c, "tp", [(i, i ^ k) for i in range(8)]) for k in range(1, 8)
    ]
    every = jnp.stack(every, axis=1).astype(jnp.float32)
    every = every.transpose(2, 0, 1, 3).reshape(ROWS, STEPS * GROUPS, 2 * STATE)
    read, pair = read_state(scan_state, every[:, :, :STATE], every[:, :, STATE:], mask)

    second = product(front[:, 384:])
    (scanned,) = call(
        scan_kernel,
        [((STEPS, ROWS, SPAN), jnp.float32)],
        second[:FLAT], swap(second[FLAT:]), stored_heads, head_taps, read, pair, dt, spread, params,
    )
    third = product(gate)
    gated, squares = call(
        gate_kernel,
        [((STEPS, ROWS, SPAN), jnp.float32), ((STEPS, GROUPS, ROWS), jnp.float32)],
        third[:FLAT], swap(third[FLAT:]), scanned, member,
    )
    for k in (1, 2, 4):
        squares = squares + lax.ppermute(squares, "tp", [(i, i ^ k) for i in range(8)])
    (mixer_out,) = call(
        norm_kernel, [((STEPS, ROWS, SPAN), jnp.bfloat16)], gated, squares, member, gain
    )
    return mixer_out


def solution(mesh):
    return jax.shard_map(
        per_device,
        mesh=mesh,
        in_specs=(
            P(("fsdp", "tp"), None),
            P(("fsdp", "tp"), None),
            P(("fsdp", "tp"), None),
            P(("fsdp", "tp"), None),
            P(None, ("fsdp", "tp")),
            P(None, ("fsdp", "tp")),
            P(None, ("fsdp", "tp")),
            P(None, ("fsdp", "tp")),
            P(),
            P(),
            P(),
            P(),
            P(None, "fsdp", None),
            P("fsdp", "tp", None, None),
            P("fsdp", None, "tp"),
            P("fsdp", None, None, "tp", None),
            P(),
            P(),
            P(),
            P(),
        ),
        out_specs=P(None, "fsdp", "tp"),
        check_vma=False,
    )
```

```python
import functools

import jax
import jax.numpy as jnp
from jax import lax
from jax.experimental import pallas as pl
from jax.experimental.pallas import tpu as pltpu
from jax.sharding import Mesh
from jax.sharding import PartitionSpec as P

TAPS = 4
ADAM_STEP = 100
STEPS = 3
ROWS = 48
FLAT = STEPS * ROWS
HEADS = 128
GROUPS = 8
HEAD_DIM = 64
STATE = 128
OWN_HEADS = 16
SPAN = OWN_HEADS * HEAD_DIM
JOINED = 18560
PIECE = 3712
PIECES = JOINED // PIECE
SHARD = 80
INNER = HEADS * HEAD_DIM

beta_one = 0.9
beta_two = 0.95
adam_eps = 1e-08
weight_decay = 0.1
norm_eps = 1e-05
HIGH = lax.Precision.HIGHEST


def adamw(master, gradient, first, second, rate):
    slope = gradient.astype(jnp.float32)
    moment_one = beta_one * first + (1.0 - beta_one) * slope
    moment_two = beta_two * second + (1.0 - beta_two) * slope * slope
    fixed_one = moment_one / (1.0 - beta_one**ADAM_STEP)
    fixed_two = moment_two / (1.0 - beta_two**ADAM_STEP)
    update = fixed_one / (jnp.sqrt(fixed_two) + adam_eps) + weight_decay * master
    return (master - rate * update).astype(jnp.bfloat16)


def refit_kernel(
    ints, order, rate, conv_m, conv_g, conv_f, conv_s, master, grad, first, second,
    out, work, m, g, f, s, sems,
):
    copies = []
    for p in range(PIECES):
        cols = pl.ds(p * PIECE, PIECE)
        copies.append(
            [
                pltpu.make_async_copy(hbm.at[:, cols], vmem.at[:, cols], sems.at[p, i])
                for i, (hbm, vmem) in enumerate(((master, m), (grad, g), (first, f), (second, s)))
            ]
        )
    for piece in copies:
        for copy in piece:
            copy.start()
    for p, piece in enumerate(copies):
        for copy in piece:
            copy.wait()
        for j in range(p * PIECE, (p + 1) * PIECE, 128):
            cols = slice(j, j + 128)
            work[:, cols] = adamw(m[:, cols], g[:, cols], f[:, cols], s[:, cols], rate[...]).astype(jnp.float32)

    lane = lax.broadcasted_iota(jnp.int32, (32, 128), 1)
    conv = adamw(conv_m[...], conv_g[...], conv_f[...], conv_s[...], rate[...])
    shift = lax.broadcasted_iota(jnp.int32, (SHARD, 128), 1) - lax.broadcasted_iota(jnp.int32, (SHARD, 128), 0) == 16
    conv = jnp.dot(conv, shift.astype(jnp.bfloat16), preferred_element_type=jnp.float32)
    conv = jnp.concatenate([conv, jnp.zeros((27, 128), jnp.float32)], axis=0)
    offsets = [ints[HEADS + GROUPS + i] for i in range(5)]
    dt = work[:, pl.ds(pl.multiple_of(offsets[4], 128), 128)]
    onehot = (lax.broadcasted_iota(jnp.int32, (HEADS, HEADS), 0) == order[...]).astype(jnp.bfloat16)
    dt = jnp.dot(dt.astype(jnp.bfloat16), onehot, preferred_element_type=jnp.float32)

    def block(start):
        return work[:, pl.ds(pl.multiple_of(start, 128), 128)]

    def half(start, head, low):
        wide = block(start + (head // 2) * 128)
        turn = (head % 2) != (0 if low else 1)
        return jnp.where(turn, pltpu.roll(wide, 64, 1), wide)

    for owner in range(8):
        group = ints[HEADS + owner]
        mine = dt if owner == 0 else pltpu.roll(dt, 128 - 16 * owner, 1)
        leading = (block(offsets[2] + group * 128), block(offsets[3] + group * 128), jnp.where(lane < 16, mine, 0.0), conv)
        for quarter in range(4):
            to = quarter * 8 + owner
            out[to, :, 0:128] = leading[quarter].astype(jnp.bfloat16)
            for k in range(2):
                low = ints[owner * OWN_HEADS + 4 * quarter + 2 * k]
                high = ints[owner * OWN_HEADS + 4 * quarter + 2 * k + 1]
                for segment, at in ((1, 128), (0, 384)):
                    start = offsets[segment]
                    both = jnp.where(lane < 64, half(start, low, True), half(start, high, False))
                    out[to, :, at + k * 128 : at + (k + 1) * 128] = both.astype(jnp.bfloat16)


def refit(rate, ints, order, conv, weight):
    vmem = pl.BlockSpec(memory_space=pltpu.VMEM)
    hbm = pl.BlockSpec(memory_space=pltpu.HBM)
    return pl.pallas_call(
        refit_kernel,
        in_specs=[pl.BlockSpec(memory_space=pltpu.SMEM)] + [vmem] * 6 + [hbm] * 4,
        out_specs=vmem,
        out_shape=jax.ShapeDtypeStruct((32, 32, 640), jnp.bfloat16),
        scratch_shapes=[
            pltpu.VMEM((32, JOINED), jnp.float32),
            pltpu.VMEM((32, JOINED), jnp.float32),
            pltpu.VMEM((32, JOINED), jnp.bfloat16),
            pltpu.VMEM((32, JOINED), jnp.float32),
            pltpu.VMEM((32, JOINED), jnp.float32),
            pltpu.SemaphoreType.DMA((PIECES, 4)),
        ],
        compiler_params=pltpu.CompilerParams(vmem_limit_bytes=58 * 2**20),
        name="refit",
    )(ints, order, rate.reshape(1, 1), *conv, *weight)


def tables_kernel(place, ints, decay, bias, skip, gain, lanes, member, mask, spread):
    owner = place[0]
    lane = lax.broadcasted_iota(jnp.int32, (1, 128), 1)
    heads = []
    for k in range(8):
        low = ints[owner * OWN_HEADS + 2 * k]
        high = ints[owner * OWN_HEADS + 2 * k + 1]
        heads.append(jnp.where(lane < 64, low, high))
        halves = []
        for head, odd in ((low, 0), (high, 1)):
            wide = gain[:, pl.ds(pl.multiple_of(head // 2 * 128, 128), 128)]
            halves.append(jnp.where(head % 2 != odd, pltpu.roll(wide, 64, 1), wide))
        lanes[3:4, k * 128 : (k + 1) * 128] = jnp.where(lane < 64, halves[0], halves[1])
    heads = jnp.concatenate(heads, axis=1)
    onehot = (lax.broadcasted_iota(jnp.int32, (HEADS, SPAN), 0) == heads).astype(jnp.float32)
    rows = jnp.concatenate([-jnp.exp(decay[...]), bias[...], skip[...], jnp.zeros((5, HEADS), jnp.float32)], axis=0)
    lanes[0:3, :] = jnp.dot(rows, onehot, precision=HIGH, preferred_element_type=jnp.float32)[0:3]
    group = heads // OWN_HEADS
    member[...] = (lax.broadcasted_iota(jnp.int32, (GROUPS, SPAN), 0) == group).astype(jnp.float32)
    for k in range(GROUPS):
        partner = lax.rem(owner // 4 * 4 + k // 4 * 4, 8) + lax.rem(owner + k, 4)
        mask[k : k + 1, :] = (group == ints[HEADS + partner]).astype(jnp.float32)
    slot = lax.broadcasted_iota(jnp.int32, (128, SPAN), 1) // HEAD_DIM
    spread[...] = (lax.broadcasted_iota(jnp.int32, (128, SPAN), 0) == slot).astype(jnp.bfloat16)


def multiply(place, rows, weights, outs):
    total = None
    for n, turn in enumerate((0, 3, 1, 2)):
        at = lax.rem(place[2] + turn, 4)
        cols = [pl.ds(pl.multiple_of((x * 4 + at) * 512, 512), 512) for x in range(2)]
        left = jnp.concatenate([jnp.concatenate([ref[:, c] for c in cols], axis=1) for ref in rows], axis=0)
        right = jnp.concatenate([part[...] for part in weights[n]], axis=0)
        term = jnp.dot(left, right, preferred_element_type=jnp.float32)
        total = term if total is None else total + term
    for i, out in enumerate(outs):
        out[0:FLAT, :] = total[i * FLAT : (i + 1) * FLAT].astype(jnp.bfloat16)


def wide_product_kernel(place, *refs):
    top, bottom, left_top, right_bottom, from_left, from_right = refs[6:12]
    halves = lambda ref: (ref.at[0:512, :], ref.at[512:1024, :])
    left_bottom, far_top = halves(from_left)
    right_top, far_bottom = halves(from_right)
    weights = ((top, bottom), (left_top, left_bottom), (right_top, right_bottom), (far_top, far_bottom))
    multiply(place, refs[:6], weights, refs[12:16])


def first_product_kernel(place, ints, *refs):
    buffers, outs, shards = refs[6:10], refs[10:14], refs[14]
    multiply(place, refs[:6], [(ref,) for ref in buffers], outs)
    owner, z = place[0], place[2]
    row = 0
    for piece in buffers:
        for t in range(piece.shape[0] // 32):
            shards[row : row + 8, :] = piece[t * 32 : t * 32 + 16, :].astype(jnp.float32)[:8]
            row += 8
    lane = lax.broadcasted_iota(jnp.int32, (8, 128), 1)

    def shard(device, shift):
        device = jnp.minimum(device, 127)
        turn = lax.rem(device // 16 % 4 + 4 - z, 4)
        at = jnp.where(turn == 0, 0, jnp.where(turn == 3, 1, turn + 1)) * 32
        at = (at + device // 64 * 16 + device % 16) * 8
        return pltpu.roll(shards[pl.ds(pl.multiple_of(at, 8), 8), :], lax.rem(shift, 128), 1)

    def unit(u, at):
        device = 4 * u // 5
        offset = 64 * u - 80 * device
        low = shard(device, at + 240 - offset)
        high = shard(device + 1, at + 192 - offset)
        return jnp.where(lane - at < 80 - offset, low, high)

    blocks = []
    for block in range(10):
        if block < 8:
            units = [ints[owner * OWN_HEADS + 2 * block + i] for i in range(2)]
        else:
            units = [HEADS + 16 * (block - 8) + 2 * ints[HEADS + owner] + i for i in range(2)]
        blocks.append(jnp.where(lane < 64, unit(units[0], 0), unit(units[1], 64)))
    taps = jnp.concatenate(blocks, axis=0).astype(jnp.bfloat16)
    for out in outs:
        out[FLAT : FLAT + 80, :] = taps


def silu(value):
    return value * jax.nn.sigmoid(value)


def convolve(inputs, stored, taps):
    window = [stored[j].astype(jnp.float32) for j in range(TAPS - 1)] + inputs
    outputs = []
    for moment in range(STEPS):
        total = taps[TAPS : TAPS + 1]
        for lag in range(TAPS):
            total = total + taps[lag : lag + 1] * window[moment + lag]
        outputs.append(silu(total).astype(jnp.bfloat16))
    return outputs


def gathered(place, pieces, buffer):
    quarter = 2 * place[1] + place[3]
    width = min(pieces[0].shape[1], 256)
    for i, piece in enumerate(pieces):
        for part in range(piece.shape[1] // width):
            at = pl.multiple_of(lax.bitwise_xor(quarter, i) * width + part * SPAN, 128)
            buffer[:, pl.ds(at, width)] = piece[:, part * width : (part + 1) * width]
    return [buffer[t * ROWS : (t + 1) * ROWS, :].astype(jnp.float32) for t in range(STEPS)]


def groups_kernel(place, *refs):
    pieces, (stored, out, dt, head_taps, buffer) = refs[:4], refs[4:]
    values = gathered(place, pieces, buffer)
    taps = buffer[FLAT : FLAT + 80, 384:512].astype(jnp.float32)
    for block in range(8):
        head_taps[:, block * 128 : (block + 1) * 128] = taps[block * 8 : block * 8 + 8]
    taps = jnp.concatenate([taps[64:72], taps[72:80]], axis=1)
    for t, value in enumerate(convolve([value[:, :256] for value in values], stored, taps)):
        out[t] = value
        dt[t] = values[t][:, 256:384].astype(jnp.bfloat16)


def state_kernel(state, every, c_all, mask, out, pair):
    chosen = mask[...]
    for r in range(8):
        read = lax.dot_general(
            c_all[r].astype(jnp.bfloat16),
            state[r].reshape(SPAN, STATE),
            (((1,), (1,)), ((), ())),
            preferred_element_type=jnp.float32,
        )
        for t in range(STEPS):
            rows = slice(8 * t, 8 * t + 8)
            out[t, r : r + 1, :] = jnp.sum(read[rows] * chosen, axis=0, keepdims=True)
    n = 0
    for t in range(STEPS):
        for s in range(t + 1):
            total = None
            for k in range(GROUPS):
                both = every[k, t, :, STATE:] * every[k, s, :, :STATE]
                term = jnp.sum(both, axis=1, keepdims=True) * mask[k : k + 1, :]
                total = term if total is None else total + term
            pair[n] = total
            n += 1


def scan_kernel(place, *refs):
    pieces, (stored, taps, read, pair, dt, spread, params, member, gated, squares, buffer) = refs[:4], refs[4:]
    both = gathered(place, pieces, buffer)
    inputs = [value[:, :SPAN] for value in both]
    values = [v.astype(jnp.float32) for v in convolve(inputs, stored, taps[...])]
    rate = params[0:1]
    bias = params[1:2]
    skip = params[2:3]
    keeps, driven = [], []
    for t in range(STEPS):
        raw = jnp.dot(dt[t], spread[...], preferred_element_type=jnp.float32)
        delta = jax.nn.softplus(raw + bias)
        keeps.append(jnp.exp(delta * rate))
        driven.append(delta * values[t])
    n = 0
    for t in range(STEPS):
        total = skip * values[t]
        offset = n + t
        after = None
        for s in range(t, -1, -1):
            term = pair[offset] * driven[s]
            total = total + (term if after is None else after * term)
            after = keeps[s] if after is None else after * keeps[s]
            offset -= 1
        value = (total + after * read[t]) * silu(both[t][:, SPAN:])
        gated[t] = value
        squares[t] = lax.dot_general(
            member[...], value * value, (((1,), (1,)), ((), ())), precision=HIGH, preferred_element_type=jnp.float32
        )
        n += t + 1


def norm_kernel(gated, squares, member, params, out):
    for t in range(STEPS):
        scale = lax.rsqrt(squares[t] / SPAN + norm_eps)
        lanes = lax.dot_general(
            scale, member[...], (((0,), (0,)), ((), ())), precision=HIGH, preferred_element_type=jnp.float32
        )
        out[t] = (gated[t] * lanes * params[3:4]).astype(jnp.bfloat16)


def call(kernel, shapes, *args, scalars=0, scratch=()):
    vmem = pl.BlockSpec(memory_space=pltpu.VMEM)
    smem = pl.BlockSpec(memory_space=pltpu.SMEM)
    return pl.pallas_call(
        kernel,
        in_specs=[smem] * scalars + [vmem] * (len(args) - scalars),
        out_specs=[vmem] * len(shapes),
        out_shape=[jax.ShapeDtypeStruct(s, d) for s, d in shapes],
        scratch_shapes=scratch,
        compiler_params=pltpu.CompilerParams(vmem_limit_bytes=32 * 2**20),
        name=kernel.__name__,
    )(*args)


def read_state(state, every, c_all, mask):
    return pl.pallas_call(
        state_kernel,
        grid=(ROWS // 8,),
        in_specs=[
            pl.BlockSpec((8, OWN_HEADS, HEAD_DIM, STATE), lambda i: (i, 0, 0, 0)),
            pl.BlockSpec((GROUPS, STEPS, 8, 2 * STATE), lambda i: (0, 0, i, 0)),
            pl.BlockSpec((8, 24, STATE), lambda i: (i, 0, 0)),
            pl.BlockSpec((8, SPAN), lambda i: (0, 0)),
        ],
        out_specs=[
            pl.BlockSpec((3, 8, SPAN), lambda i: (0, i, 0)),
            pl.BlockSpec((6, 8, SPAN), lambda i: (0, i, 0)),
        ],
        out_shape=[
            jax.ShapeDtypeStruct((3, ROWS, SPAN), jnp.float32),
            jax.ShapeDtypeStruct((6, ROWS, SPAN), jnp.float32),
        ],
        compiler_params=pltpu.CompilerParams(vmem_limit_bytes=20 * 2**20),
        name="read_state",
    )(state, every, c_all, mask)


def per_device(
    weight_master,
    weight_grad,
    weight_first,
    weight_second,
    conv_master,
    conv_grad,
    conv_first,
    conv_second,
    learn_rate,
    segment_offsets,
    head_order,
    group_order,
    hidden_input,
    scan_state,
    conv_heads,
    conv_groups,
    decay_log,
    delta_bias,
    skip_gain,
    norm_gain,
):
    owner = lax.axis_index("tp")
    side, z, core = lax.axis_index("x"), lax.axis_index("z"), lax.axis_index("c")
    up = lambda value: lax.ppermute(value, "z", [(i, (i + 1) % 4) for i in range(4)])
    down = lambda value: lax.ppermute(value, "z", [(i, (i + 3) % 4) for i in range(4)])

    def swap(value, turn):
        return lax.ppermute(value, ("x", "c"), [(i, i ^ turn) for i in range(4)])

    position = jnp.stack([owner, side, z, core]).astype(jnp.int32)
    ints = jnp.concatenate([head_order, group_order, segment_offsets])
    def after(value, *others):
        return lax.optimization_barrier((value, *others))[0]

    far = [swap(hidden_input[0], 2)]
    near = swap(hidden_input.reshape(FLAT, -1), 1)

    sent = refit(
        learn_rate, ints, head_order.reshape(1, HEADS),
        (conv_master, conv_grad, conv_first, conv_second),
        (weight_master, weight_grad, weight_first, weight_second),
    )
    owned = lax.all_to_all(after(sent, *far, near), ("x", "c", "tp"), split_axis=0, concat_axis=0, tiled=True)
    owned = owned.reshape(1024, 640)
    far.append(swap(after(hidden_input[1:].reshape(2 * ROWS, -1), owned), 2))

    def exchanged(outs):
        return [outs[0]] + [swap(outs[i], i) for i in range(1, 4)]

    row = lambda value: value.reshape(1, -1)
    params, member, mask, spread = call(
        tables_kernel,
        [
            ((8, SPAN), jnp.float32),
            ((GROUPS, SPAN), jnp.float32),
            ((GROUPS, SPAN), jnp.float32),
            ((128, SPAN), jnp.bfloat16),
        ],
        position, after(ints, sent), row(decay_log), row(delta_bias), row(skip_gain), row(norm_gain), scalars=2,
    )
    stored_heads = jnp.swapaxes(conv_heads, 0, 1)
    stored_groups = jnp.swapaxes(conv_groups.reshape(ROWS, TAPS - 1, 2 * STATE), 0, 1)

    own = owned[:, :128]
    pieces = [own, up(own), down(own), lax.ppermute(own, "z", [(i, (i + 2) % 4) for i in range(4)])]
    far_pair = after(far, *pieces[1:])
    rows = [hidden_input.reshape(FLAT, -1), near, *far, *[swap(value, 1) for value in far_pair]]
    top, bottom = [after(owned[512 * i : 512 * i + 512, 128:], *pieces[1:]) for i in range(2)]
    left_top, right_bottom = up(top), down(bottom)

    first = call(
        first_product_kernel, [((FLAT + 80, 128), jnp.bfloat16)] * 4, position, ints, *rows, *pieces,
        scalars=2, scratch=[pltpu.VMEM((1024, 128), jnp.float32)],
    )
    arrived = after((left_top, right_bottom), first)
    from_left = up(jnp.concatenate([bottom, arrived[0]]))
    from_right = down(jnp.concatenate([top, arrived[1]]))
    b_and_c, dt, head_taps = call(
        groups_kernel,
        [((STEPS, ROWS, 2 * STATE), jnp.bfloat16), ((STEPS, ROWS, 128), jnp.bfloat16), ((8, SPAN), jnp.float32)],
        position, *exchanged(first), stored_groups, scalars=1, scratch=[pltpu.VMEM((FLAT + 80, 512), jnp.bfloat16)],
    )
    ahead = lambda k: [(i, i // 4 * 4 + (i + 4 - k) % 4) for i in range(8)]
    every = jnp.stack([b_and_c] + [lax.ppermute(b_and_c, "tp", ahead(k)) for k in range(1, 4)])
    every = jnp.concatenate([every, lax.ppermute(every, "tp", [(i, i ^ 4) for i in range(8)])])
    every = every.astype(jnp.float32)
    c_all = every[..., STATE:].transpose(2, 1, 0, 3).reshape(ROWS, STEPS * GROUPS, STATE)
    read, pair = read_state(scan_state, every, c_all, mask)

    second = exchanged(
        call(
            wide_product_kernel, [((FLAT, 512), jnp.bfloat16)] * 4, position, *rows,
            after(top, read), bottom, left_top, right_bottom, from_left, from_right,
            scalars=1,
        )
    )
    gated, squares = call(
        scan_kernel,
        [((STEPS, ROWS, SPAN), jnp.float32), ((STEPS, GROUPS, ROWS), jnp.float32)],
        position, *second, stored_heads, head_taps, read, pair, dt, spread, params, member,
        scalars=1, scratch=[pltpu.VMEM((FLAT, 2 * SPAN), jnp.bfloat16)],
    )
    for k in (1, 2, 4):
        squares = squares + lax.ppermute(squares, "tp", [(i, i ^ k) for i in range(8)])
    (mixer_out,) = call(
        norm_kernel, [((STEPS, ROWS, SPAN), jnp.bfloat16)], gated, squares, member, params
    )
    return mixer_out


def solution(mesh):
    mesh = Mesh(mesh.devices.reshape(2, 4, 2, 8), ("x", "z", "c", "tp"))
    fsdp = ("x", "z", "c")
    every = fsdp + ("tp",)
    return jax.shard_map(
        per_device,
        mesh=mesh,
        in_specs=(P(every, None),) * 4
        + (P(None, every),) * 4
        + (P(),) * 4
        + (P(None, fsdp, None), P(fsdp, "tp", None, None), P(fsdp, None, "tp"), P(fsdp, None, None, "tp", None))
        + (P(),) * 4,
        out_specs=P(None, fsdp, "tp"),
        check_vma=False,
    )
```

```python
import functools

import jax
import jax.numpy as jnp
from jax import lax
from jax.experimental import pallas as pl
from jax.experimental.pallas import tpu as pltpu
from jax.sharding import Mesh
from jax.sharding import PartitionSpec as P

TAPS = 4
ADAM_STEP = 100
STEPS = 3
ROWS = 48
FLAT = STEPS * ROWS
HEADS = 128
GROUPS = 8
HEAD_DIM = 64
STATE = 128
OWN_HEADS = 16
SPAN = OWN_HEADS * HEAD_DIM
JOINED = 18560
PIECE = 3712
PIECES = JOINED // PIECE
SHARD = 80
INNER = HEADS * HEAD_DIM

beta_one = 0.9
beta_two = 0.95
adam_eps = 1e-08
weight_decay = 0.1
norm_eps = 1e-05
HIGH = lax.Precision.HIGHEST


def adamw(master, gradient, first, second, rate):
    slope = gradient.astype(jnp.float32)
    moment_one = beta_one * first + (1.0 - beta_one) * slope
    moment_two = beta_two * second + (1.0 - beta_two) * slope * slope
    fixed_one = moment_one / (1.0 - beta_one**ADAM_STEP)
    fixed_two = moment_two / (1.0 - beta_two**ADAM_STEP)
    update = fixed_one / (jnp.sqrt(fixed_two) + adam_eps) + weight_decay * master
    return (master - rate * update).astype(jnp.bfloat16)


def refit_kernel(
    ints, order, rate, conv_m, conv_g, conv_f, conv_s, master, grad, first, second,
    out, work, m, g, f, s, sems,
):
    copies = []
    for p in range(PIECES):
        cols = pl.ds(p * PIECE, PIECE)
        copies.append(
            [
                pltpu.make_async_copy(hbm.at[:, cols], vmem.at[:, cols], sems.at[p, i])
                for i, (hbm, vmem) in enumerate(((master, m), (grad, g), (first, f), (second, s)))
            ]
        )
    for piece in copies:
        for copy in piece:
            copy.start()
    for p, piece in enumerate(copies):
        for copy in piece:
            copy.wait()
        for j in range(p * PIECE, (p + 1) * PIECE, 128):
            cols = slice(j, j + 128)
            work[:, cols] = adamw(m[:, cols], g[:, cols], f[:, cols], s[:, cols], rate[...]).astype(jnp.float32)

    lane = lax.broadcasted_iota(jnp.int32, (32, 128), 1)
    conv = adamw(conv_m[...], conv_g[...], conv_f[...], conv_s[...], rate[...])
    shift = lax.broadcasted_iota(jnp.int32, (SHARD, 128), 1) - lax.broadcasted_iota(jnp.int32, (SHARD, 128), 0) == 16
    conv = jnp.dot(conv, shift.astype(jnp.bfloat16), preferred_element_type=jnp.float32)
    conv = jnp.concatenate([conv, jnp.zeros((27, 128), jnp.float32)], axis=0)
    offsets = [ints[HEADS + GROUPS + i] for i in range(5)]
    dt = work[:, pl.ds(pl.multiple_of(offsets[4], 128), 128)]
    onehot = (lax.broadcasted_iota(jnp.int32, (HEADS, HEADS), 0) == order[...]).astype(jnp.bfloat16)
    dt = jnp.dot(dt.astype(jnp.bfloat16), onehot, preferred_element_type=jnp.float32)

    def block(start):
        return work[:, pl.ds(pl.multiple_of(start, 128), 128)]

    def half(start, head, low):
        wide = block(start + (head // 2) * 128)
        turn = (head % 2) != (0 if low else 1)
        return jnp.where(turn, pltpu.roll(wide, 64, 1), wide)

    for owner in range(8):
        group = ints[HEADS + owner]
        mine = dt if owner == 0 else pltpu.roll(dt, 128 - 16 * owner, 1)
        leading = (block(offsets[2] + group * 128), block(offsets[3] + group * 128), jnp.where(lane < 16, mine, 0.0), conv)
        for quarter in range(4):
            to = quarter * 8 + owner
            out[to, :, 0:128] = leading[quarter].astype(jnp.bfloat16)
            for k in range(2):
                low = ints[owner * OWN_HEADS + 4 * quarter + 2 * k]
                high = ints[owner * OWN_HEADS + 4 * quarter + 2 * k + 1]
                for segment, at in ((1, 128), (0, 384)):
                    start = offsets[segment]
                    both = jnp.where(lane < 64, half(start, low, True), half(start, high, False))
                    out[to, :, at + k * 128 : at + (k + 1) * 128] = both.astype(jnp.bfloat16)


def refit(rate, ints, order, conv, weight):
    vmem = pl.BlockSpec(memory_space=pltpu.VMEM)
    hbm = pl.BlockSpec(memory_space=pltpu.HBM)
    return pl.pallas_call(
        refit_kernel,
        in_specs=[pl.BlockSpec(memory_space=pltpu.SMEM)] + [vmem] * 6 + [hbm] * 4,
        out_specs=vmem,
        out_shape=jax.ShapeDtypeStruct((32, 32, 640), jnp.bfloat16),
        scratch_shapes=[
            pltpu.VMEM((32, JOINED), jnp.float32),
            pltpu.VMEM((32, JOINED), jnp.float32),
            pltpu.VMEM((32, JOINED), jnp.bfloat16),
            pltpu.VMEM((32, JOINED), jnp.float32),
            pltpu.VMEM((32, JOINED), jnp.float32),
            pltpu.SemaphoreType.DMA((PIECES, 4)),
        ],
        compiler_params=pltpu.CompilerParams(vmem_limit_bytes=58 * 2**20),
        name="refit",
    )(ints, order, rate.reshape(1, 1), *conv, *weight)


def tables_kernel(place, ints, decay, bias, skip, gain, lanes, member, mask, spread):
    owner = place[0]
    lane = lax.broadcasted_iota(jnp.int32, (1, 128), 1)
    heads = []
    for k in range(8):
        low = ints[owner * OWN_HEADS + 2 * k]
        high = ints[owner * OWN_HEADS + 2 * k + 1]
        heads.append(jnp.where(lane < 64, low, high))
        halves = []
        for head, odd in ((low, 0), (high, 1)):
            wide = gain[:, pl.ds(pl.multiple_of(head // 2 * 128, 128), 128)]
            halves.append(jnp.where(head % 2 != odd, pltpu.roll(wide, 64, 1), wide))
        lanes[3:4, k * 128 : (k + 1) * 128] = jnp.where(lane < 64, halves[0], halves[1])
    heads = jnp.concatenate(heads, axis=1)
    onehot = (lax.broadcasted_iota(jnp.int32, (HEADS, SPAN), 0) == heads).astype(jnp.float32)
    rows = jnp.concatenate([-jnp.exp(decay[...]), bias[...], skip[...], jnp.zeros((5, HEADS), jnp.float32)], axis=0)
    lanes[0:3, :] = jnp.dot(rows, onehot, precision=HIGH, preferred_element_type=jnp.float32)[0:3]
    group = heads // OWN_HEADS
    member[...] = (lax.broadcasted_iota(jnp.int32, (GROUPS, SPAN), 0) == group).astype(jnp.float32)
    for k in range(GROUPS):
        partner = lax.rem(owner // 4 * 4 + k // 4 * 4, 8) + lax.rem(owner + k, 4)
        mask[k : k + 1, :] = (group == ints[HEADS + partner]).astype(jnp.float32)
    slot = lax.broadcasted_iota(jnp.int32, (128, SPAN), 1) // HEAD_DIM
    spread[...] = (lax.broadcasted_iota(jnp.int32, (128, SPAN), 0) == slot).astype(jnp.bfloat16)


def multiply(place, rows, weights, outs):
    total = None
    for n, turn in enumerate((0, 3, 1, 2)):
        at = lax.rem(place[2] + turn, 4)
        cols = [pl.ds(pl.multiple_of((x * 4 + at) * 512, 512), 512) for x in range(2)]
        left = jnp.concatenate([jnp.concatenate([ref[:, c] for c in cols], axis=1) for ref in rows], axis=0)
        right = jnp.concatenate([part[...] for part in weights[n]], axis=0)
        term = jnp.dot(left, right, preferred_element_type=jnp.float32)
        total = term if total is None else total + term
    for i, out in enumerate(outs):
        out[0:FLAT, :] = total[i * FLAT : (i + 1) * FLAT].astype(jnp.bfloat16)


def wide_product_kernel(place, *refs):
    top, bottom, left_top, right_bottom, from_left, from_right = refs[6:12]
    halves = lambda ref: (ref.at[0:512, :], ref.at[512:1024, :])
    left_bottom, far_top = halves(from_left)
    right_top, far_bottom = halves(from_right)
    weights = ((top, bottom), (left_top, left_bottom), (right_top, right_bottom), (far_top, far_bottom))
    multiply(place, refs[:6], weights, refs[12:16])


def first_product_kernel(place, ints, *refs):
    buffers, outs, shards = refs[6:10], refs[10:14], refs[14]
    multiply(place, refs[:6], [(ref,) for ref in buffers], outs)
    owner, z = place[0], place[2]
    row = 0
    for piece in buffers:
        for t in range(piece.shape[0] // 32):
            shards[row : row + 8, :] = piece[t * 32 : t * 32 + 16, :].astype(jnp.float32)[:8]
            row += 8
    lane = lax.broadcasted_iota(jnp.int32, (8, 128), 1)

    def shard(device, shift):
        device = jnp.minimum(device, 127)
        turn = lax.rem(device // 16 % 4 + 4 - z, 4)
        at = jnp.where(turn == 0, 0, jnp.where(turn == 3, 1, turn + 1)) * 32
        at = (at + device // 64 * 16 + device % 16) * 8
        return pltpu.roll(shards[pl.ds(pl.multiple_of(at, 8), 8), :], lax.rem(shift, 128), 1)

    def unit(u, at):
        device = 4 * u // 5
        offset = 64 * u - 80 * device
        low = shard(device, at + 240 - offset)
        high = shard(device + 1, at + 192 - offset)
        return jnp.where(lane - at < 80 - offset, low, high)

    blocks = []
    for block in range(10):
        if block < 8:
            units = [ints[owner * OWN_HEADS + 2 * block + i] for i in range(2)]
        else:
            units = [HEADS + 16 * (block - 8) + 2 * ints[HEADS + owner] + i for i in range(2)]
        blocks.append(jnp.where(lane < 64, unit(units[0], 0), unit(units[1], 64)))
    taps = jnp.concatenate(blocks, axis=0).astype(jnp.bfloat16)
    for out in outs:
        out[FLAT : FLAT + 80, :] = taps


def silu(value):
    return value * jax.nn.sigmoid(value)


def convolve(inputs, stored, taps):
    window = [stored[j].astype(jnp.float32) for j in range(TAPS - 1)] + inputs
    outputs = []
    for moment in range(STEPS):
        total = taps[TAPS : TAPS + 1]
        for lag in range(TAPS):
            total = total + taps[lag : lag + 1] * window[moment + lag]
        outputs.append(silu(total).astype(jnp.bfloat16))
    return outputs


def gathered(place, pieces, buffer):
    quarter = 2 * place[1] + place[3]
    width = min(pieces[0].shape[1], 256)
    for i, piece in enumerate(pieces):
        for part in range(piece.shape[1] // width):
            at = pl.multiple_of(lax.bitwise_xor(quarter, i) * width + part * SPAN, 128)
            buffer[:, pl.ds(at, width)] = piece[:, part * width : (part + 1) * width]
    return [buffer[t * ROWS : (t + 1) * ROWS, :].astype(jnp.float32) for t in range(STEPS)]


def groups_kernel(place, *refs):
    pieces, (stored, out, dt, head_taps, buffer) = refs[:4], refs[4:]
    values = gathered(place, pieces, buffer)
    taps = buffer[FLAT : FLAT + 80, 384:512].astype(jnp.float32)
    for block in range(8):
        head_taps[:, block * 128 : (block + 1) * 128] = taps[block * 8 : block * 8 + 8]
    taps = jnp.concatenate([taps[64:72], taps[72:80]], axis=1)
    for t, value in enumerate(convolve([value[:, :256] for value in values], stored, taps)):
        out[t] = value
        dt[t] = values[t][:, 256:384].astype(jnp.bfloat16)


def state_kernel(state, every, c_all, mask, out, pair):
    chosen = mask[...]
    for r in range(8):
        read = lax.dot_general(
            c_all[r].astype(jnp.bfloat16),
            state[r].reshape(SPAN, STATE),
            (((1,), (1,)), ((), ())),
            preferred_element_type=jnp.float32,
        )
        for t in range(STEPS):
            rows = slice(8 * t, 8 * t + 8)
            out[t, r : r + 1, :] = jnp.sum(read[rows] * chosen, axis=0, keepdims=True)
    n = 0
    for t in range(STEPS):
        for s in range(t + 1):
            total = None
            for k in range(GROUPS):
                both = every[k, t, :, STATE:] * every[k, s, :, :STATE]
                term = jnp.sum(both, axis=1, keepdims=True) * mask[k : k + 1, :]
                total = term if total is None else total + term
            pair[n] = total
            n += 1


def scan_kernel(place, *refs):
    pieces, (stored, taps, *refs) = refs[:4], refs[4:]
    read, read_more, pair, pair_more, dt, spread, params, member, gated, squares, buffer = refs
    whole = lambda low, high, n: jnp.concatenate([low[n], high[n]], axis=0)
    both = gathered(place, pieces, buffer)
    inputs = [value[:, :SPAN] for value in both]
    values = [v.astype(jnp.float32) for v in convolve(inputs, stored, taps[...])]
    rate = params[0:1]
    bias = params[1:2]
    skip = params[2:3]
    keeps, driven = [], []
    for t in range(STEPS):
        raw = jnp.dot(dt[t], spread[...], preferred_element_type=jnp.float32)
        delta = jax.nn.softplus(raw + bias)
        keeps.append(jnp.exp(delta * rate))
        driven.append(delta * values[t])
    n = 0
    for t in range(STEPS):
        total = skip * values[t]
        offset = n + t
        after = None
        for s in range(t, -1, -1):
            term = whole(pair, pair_more, offset) * driven[s]
            total = total + (term if after is None else after * term)
            after = keeps[s] if after is None else after * keeps[s]
            offset -= 1
        value = (total + after * whole(read, read_more, t)) * silu(both[t][:, SPAN:])
        gated[t] = value * params[3:4]
        total = lax.dot_general(
            member[...], value * value, (((1,), (1,)), ((), ())), precision=HIGH, preferred_element_type=jnp.float32
        )
        total = jnp.concatenate([total, jnp.zeros((GROUPS, 128 - ROWS), jnp.float32)], axis=1)
        for to in range(8):
            squares[to, 8 * t : 8 * t + 8, :] = total
        n += t + 1


def norm_kernel(gated, squares, member, out):
    for t in range(STEPS):
        total = squares[0, 8 * t : 8 * t + 8, 0:ROWS]
        for owner in range(1, 8):
            total = total + squares[owner, 8 * t : 8 * t + 8, 0:ROWS]
        scale = lax.rsqrt(total / SPAN + norm_eps)
        lanes = lax.dot_general(
            scale, member[...], (((0,), (0,)), ((), ())), precision=HIGH, preferred_element_type=jnp.float32
        )
        out[t] = (gated[t] * lanes).astype(jnp.bfloat16)


def call(kernel, shapes, *args, scalars=0, scratch=(), limit=12):
    vmem = pl.BlockSpec(memory_space=pltpu.VMEM)
    smem = pl.BlockSpec(memory_space=pltpu.SMEM)
    return pl.pallas_call(
        kernel,
        in_specs=[smem] * scalars + [vmem] * (len(args) - scalars),
        out_specs=[vmem] * len(shapes),
        out_shape=[jax.ShapeDtypeStruct(s, d) for s, d in shapes],
        scratch_shapes=scratch,
        compiler_params=pltpu.CompilerParams(vmem_limit_bytes=limit * 2**20),
        name=kernel.__name__,
    )(*args)


def read_state(state, every, c_all, mask, part):
    return pl.pallas_call(
        state_kernel,
        grid=(ROWS // 16,),
        in_specs=[
            pl.BlockSpec((8, OWN_HEADS, HEAD_DIM, STATE), lambda i: (i + 3 * part, 0, 0, 0)),
            pl.BlockSpec((GROUPS, STEPS, 8, 2 * STATE), lambda i: (0, 0, i + 3 * part, 0)),
            pl.BlockSpec((8, 24, STATE), lambda i: (i + 3 * part, 0, 0)),
            pl.BlockSpec((8, SPAN), lambda i: (0, 0)),
        ],
        out_specs=[
            pl.BlockSpec((3, 8, SPAN), lambda i: (0, i, 0)),
            pl.BlockSpec((6, 8, SPAN), lambda i: (0, i, 0)),
        ],
        out_shape=[
            jax.ShapeDtypeStruct((3, ROWS // 2, SPAN), jnp.float32),
            jax.ShapeDtypeStruct((6, ROWS // 2, SPAN), jnp.float32),
        ],
        compiler_params=pltpu.CompilerParams(vmem_limit_bytes=50 * 2**20),
        name="read_state",
    )(state, every, c_all, mask)


def per_device(
    weight_master,
    weight_grad,
    weight_first,
    weight_second,
    conv_master,
    conv_grad,
    conv_first,
    conv_second,
    learn_rate,
    segment_offsets,
    head_order,
    group_order,
    hidden_input,
    scan_state,
    conv_heads,
    conv_groups,
    decay_log,
    delta_bias,
    skip_gain,
    norm_gain,
):
    owner = lax.axis_index("tp")
    side, z, core = lax.axis_index("x"), lax.axis_index("z"), lax.axis_index("c")
    up = lambda value: lax.ppermute(value, "z", [(i, (i + 1) % 4) for i in range(4)])
    down = lambda value: lax.ppermute(value, "z", [(i, (i + 3) % 4) for i in range(4)])

    def swap(value, turn):
        return lax.ppermute(value, ("x", "c"), [(i, i ^ turn) for i in range(4)])

    position = jnp.stack([owner, side, z, core]).astype(jnp.int32)
    ints = jnp.concatenate([head_order, group_order, segment_offsets])
    def after(value, *others):
        return lax.optimization_barrier((value, *others))[0]

    far = [swap(hidden_input[0], 2)]
    near = swap(hidden_input.reshape(FLAT, -1), 1)

    sent = refit(
        learn_rate, ints, head_order.reshape(1, HEADS),
        (conv_master, conv_grad, conv_first, conv_second),
        (weight_master, weight_grad, weight_first, weight_second),
    )
    owned = lax.all_to_all(after(sent, *far, near), ("x", "c", "tp"), split_axis=0, concat_axis=0, tiled=True)
    owned = owned.reshape(1024, 640)
    far.append(swap(after(hidden_input[1:].reshape(2 * ROWS, -1), owned), 2))

    def exchanged(outs):
        return [outs[0]] + [swap(outs[i], i) for i in range(1, 4)]

    row = lambda value: value.reshape(1, -1)
    params, member, mask, spread = call(
        tables_kernel,
        [
            ((8, SPAN), jnp.float32),
            ((GROUPS, SPAN), jnp.float32),
            ((GROUPS, SPAN), jnp.float32),
            ((128, SPAN), jnp.bfloat16),
        ],
        position, after(ints, sent), row(decay_log), row(delta_bias), row(skip_gain), row(norm_gain), scalars=2,
    )
    stored_heads = jnp.swapaxes(conv_heads, 0, 1)
    stored_groups = jnp.swapaxes(conv_groups.reshape(ROWS, TAPS - 1, 2 * STATE), 0, 1)

    own = owned[:, :128]
    pieces = [own, up(own), down(own), lax.ppermute(own, "z", [(i, (i + 2) % 4) for i in range(4)])]
    far_pair = after(far, *pieces[1:])
    rows = [hidden_input.reshape(FLAT, -1), near, *far, *[swap(value, 1) for value in far_pair]]
    top, bottom = [after(owned[512 * i : 512 * i + 512, 128:], *pieces[1:]) for i in range(2)]
    left_top, right_bottom = up(top), down(bottom)

    first = call(
        first_product_kernel, [((FLAT + 80, 128), jnp.bfloat16)] * 4, position, ints, *rows, *pieces,
        scalars=2, scratch=[pltpu.VMEM((1024, 128), jnp.float32)], limit=20,
    )
    arrived = after((left_top, right_bottom), first)
    from_left = up(jnp.concatenate([bottom, arrived[0]]))
    from_right = down(jnp.concatenate([top, arrived[1]]))
    b_and_c, dt, head_taps = call(
        groups_kernel,
        [((STEPS, ROWS, 2 * STATE), jnp.bfloat16), ((STEPS, ROWS, 128), jnp.bfloat16), ((8, SPAN), jnp.float32)],
        position, *exchanged(first), stored_groups, scalars=1, scratch=[pltpu.VMEM((FLAT + 80, 512), jnp.bfloat16)],
    )
    ahead = lambda k: [(i, i // 4 * 4 + (i + 4 - k) % 4) for i in range(8)]
    every = jnp.stack([b_and_c] + [lax.ppermute(b_and_c, "tp", ahead(k)) for k in range(1, 4)])
    every = jnp.concatenate([every, lax.ppermute(every, "tp", [(i, i ^ 4) for i in range(8)])])
    every = every.astype(jnp.float32)
    c_all = every[..., STATE:].transpose(2, 1, 0, 3).reshape(ROWS, STEPS * GROUPS, STATE)
    read, pair = read_state(scan_state, every, c_all, mask, 0)

    top, read = lax.optimization_barrier((top, read))
    second = call(
        wide_product_kernel, [((FLAT, 512), jnp.bfloat16)] * 4, position, *rows,
        top, bottom, left_top, right_bottom, from_left, from_right,
        scalars=1, limit=24,
    )
    c_all, *second = lax.optimization_barrier((c_all, *second))
    read_more, pair_more = read_state(scan_state, every, c_all, mask, 1)
    second = exchanged(second)
    gated, squares = call(
        scan_kernel,
        [((STEPS, ROWS, SPAN), jnp.float32), ((8, STEPS * GROUPS, 128), jnp.float32)],
        position, *second, stored_heads, head_taps, read, read_more, pair, pair_more, dt, spread, params, member,
        scalars=1, scratch=[pltpu.VMEM((FLAT, 2 * SPAN), jnp.bfloat16)], limit=20,
    )
    squares = lax.all_to_all(squares, "tp", split_axis=0, concat_axis=0, tiled=True)
    (mixer_out,) = call(
        norm_kernel, [((STEPS, ROWS, SPAN), jnp.bfloat16)], gated, squares, member
    )
    return mixer_out


def solution(mesh):
    mesh = Mesh(mesh.devices.reshape(2, 4, 2, 8), ("x", "z", "c", "tp"))
    fsdp = ("x", "z", "c")
    every = fsdp + ("tp",)
    return jax.shard_map(
        per_device,
        mesh=mesh,
        in_specs=(P(every, None),) * 4
        + (P(None, every),) * 4
        + (P(),) * 4
        + (P(None, fsdp, None), P(fsdp, "tp", None, None), P(fsdp, None, "tp"), P(fsdp, None, None, "tp", None))
        + (P(),) * 4,
        out_specs=P(None, fsdp, "tp"),
        check_vma=False,
    )
```

```python
import functools

import jax
import jax.numpy as jnp
from jax import lax
from jax.experimental import pallas as pl
from jax.experimental.pallas import tpu as pltpu
from jax.sharding import Mesh
from jax.sharding import PartitionSpec as P

TAPS = 4
ADAM_STEP = 100
STEPS = 3
ROWS = 48
FLAT = STEPS * ROWS
HEADS = 128
GROUPS = 8
HEAD_DIM = 64
STATE = 128
OWN_HEADS = 16
SPAN = OWN_HEADS * HEAD_DIM
JOINED = 18560
PIECE = 3712
PIECES = JOINED // PIECE
SHARD = 80
INNER = HEADS * HEAD_DIM

beta_one = 0.9
beta_two = 0.95
adam_eps = 1e-08
weight_decay = 0.1
norm_eps = 1e-05
HIGH = lax.Precision.HIGHEST


def adamw(master, gradient, first, second, rate):
    slope = gradient.astype(jnp.float32)
    moment_one = beta_one * first + (1.0 - beta_one) * slope
    moment_two = beta_two * second + (1.0 - beta_two) * slope * slope
    fixed_one = moment_one / (1.0 - beta_one**ADAM_STEP)
    fixed_two = moment_two / (1.0 - beta_two**ADAM_STEP)
    update = fixed_one / (jnp.sqrt(fixed_two) + adam_eps) + weight_decay * master
    return (master - rate * update).astype(jnp.bfloat16)


def refit_kernel(
    ints, order, rate, conv_m, conv_g, conv_f, conv_s, master, grad, first, second,
    out, work, m, g, f, s, sems,
):
    copies = []
    for p in range(PIECES):
        cols = pl.ds(p * PIECE, PIECE)
        copies.append(
            [
                pltpu.make_async_copy(hbm.at[:, cols], vmem.at[:, cols], sems.at[p, i])
                for i, (hbm, vmem) in enumerate(((master, m), (grad, g), (first, f), (second, s)))
            ]
        )
    for piece in copies:
        for copy in piece:
            copy.start()
    for p, piece in enumerate(copies):
        for copy in piece:
            copy.wait()
        for j in range(p * PIECE, (p + 1) * PIECE, 128):
            cols = slice(j, j + 128)
            work[:, cols] = adamw(m[:, cols], g[:, cols], f[:, cols], s[:, cols], rate[...]).astype(jnp.float32)

    lane = lax.broadcasted_iota(jnp.int32, (32, 128), 1)
    conv = adamw(conv_m[...], conv_g[...], conv_f[...], conv_s[...], rate[...])
    shift = lax.broadcasted_iota(jnp.int32, (SHARD, 128), 1) - lax.broadcasted_iota(jnp.int32, (SHARD, 128), 0) == 16
    conv = jnp.dot(conv, shift.astype(jnp.bfloat16), preferred_element_type=jnp.float32)
    conv = jnp.concatenate([conv, jnp.zeros((27, 128), jnp.float32)], axis=0)
    offsets = [ints[HEADS + GROUPS + i] for i in range(5)]
    dt = work[:, pl.ds(pl.multiple_of(offsets[4], 128), 128)]
    onehot = (lax.broadcasted_iota(jnp.int32, (HEADS, HEADS), 0) == order[...]).astype(jnp.bfloat16)
    dt = jnp.dot(dt.astype(jnp.bfloat16), onehot, preferred_element_type=jnp.float32)

    def block(start):
        return work[:, pl.ds(pl.multiple_of(start, 128), 128)]

    def half(start, head, low):
        wide = block(start + (head // 2) * 128)
        turn = (head % 2) != (0 if low else 1)
        return jnp.where(turn, pltpu.roll(wide, 64, 1), wide)

    for owner in range(8):
        group = ints[HEADS + owner]
        mine = dt if owner == 0 else pltpu.roll(dt, 128 - 16 * owner, 1)
        leading = (block(offsets[2] + group * 128), block(offsets[3] + group * 128), jnp.where(lane < 16, mine, 0.0), conv)
        for quarter in range(4):
            to = quarter * 8 + owner
            out[to, :, 0:128] = leading[quarter].astype(jnp.bfloat16)
            for k in range(2):
                low = ints[owner * OWN_HEADS + 4 * quarter + 2 * k]
                high = ints[owner * OWN_HEADS + 4 * quarter + 2 * k + 1]
                for segment, at in ((1, 128), (0, 384)):
                    start = offsets[segment]
                    both = jnp.where(lane < 64, half(start, low, True), half(start, high, False))
                    out[to, :, at + k * 128 : at + (k + 1) * 128] = both.astype(jnp.bfloat16)


def refit(rate, ints, order, conv, weight):
    vmem = pl.BlockSpec(memory_space=pltpu.VMEM)
    hbm = pl.BlockSpec(memory_space=pltpu.HBM)
    return pl.pallas_call(
        refit_kernel,
        in_specs=[pl.BlockSpec(memory_space=pltpu.SMEM)] + [vmem] * 6 + [hbm] * 4,
        out_specs=vmem,
        out_shape=jax.ShapeDtypeStruct((32, 32, 640), jnp.bfloat16),
        scratch_shapes=[
            pltpu.VMEM((32, JOINED), jnp.float32),
            pltpu.VMEM((32, JOINED), jnp.float32),
            pltpu.VMEM((32, JOINED), jnp.bfloat16),
            pltpu.VMEM((32, JOINED), jnp.float32),
            pltpu.VMEM((32, JOINED), jnp.float32),
            pltpu.SemaphoreType.DMA((PIECES, 4)),
        ],
        compiler_params=pltpu.CompilerParams(vmem_limit_bytes=58 * 2**20),
        name="refit",
    )(ints, order, rate.reshape(1, 1), *conv, *weight)


def tables_kernel(place, ints, decay, bias, skip, gain, lanes, member, mask, spread):
    owner = place[0]
    lane = lax.broadcasted_iota(jnp.int32, (1, 128), 1)
    heads = []
    for k in range(8):
        low = ints[owner * OWN_HEADS + 2 * k]
        high = ints[owner * OWN_HEADS + 2 * k + 1]
        heads.append(jnp.where(lane < 64, low, high))
        halves = []
        for head, odd in ((low, 0), (high, 1)):
            wide = gain[:, pl.ds(pl.multiple_of(head // 2 * 128, 128), 128)]
            halves.append(jnp.where(head % 2 != odd, pltpu.roll(wide, 64, 1), wide))
        lanes[3:4, k * 128 : (k + 1) * 128] = jnp.where(lane < 64, halves[0], halves[1])
    heads = jnp.concatenate(heads, axis=1)
    onehot = (lax.broadcasted_iota(jnp.int32, (HEADS, SPAN), 0) == heads).astype(jnp.float32)
    rows = jnp.concatenate([-jnp.exp(decay[...]), bias[...], skip[...], jnp.zeros((5, HEADS), jnp.float32)], axis=0)
    lanes[0:3, :] = jnp.dot(rows, onehot, precision=HIGH, preferred_element_type=jnp.float32)[0:3]
    group = heads // OWN_HEADS
    member[...] = (lax.broadcasted_iota(jnp.int32, (GROUPS, SPAN), 0) == group).astype(jnp.float32)
    for k in range(GROUPS):
        partner = lax.rem(owner // 4 * 4 + k // 4 * 4, 8) + lax.rem(owner + k, 4)
        mask[k : k + 1, :] = (group == ints[HEADS + partner]).astype(jnp.float32)
    slot = lax.broadcasted_iota(jnp.int32, (128, SPAN), 1) // HEAD_DIM
    spread[...] = (lax.broadcasted_iota(jnp.int32, (128, SPAN), 0) == slot).astype(jnp.bfloat16)


def multiply(place, rows, weights, outs):
    total = None
    for n, turn in enumerate((0, 3, 1, 2)):
        at = lax.rem(place[2] + turn, 4)
        cols = [pl.ds(pl.multiple_of((x * 4 + at) * 512, 512), 512) for x in range(2)]
        left = jnp.concatenate([jnp.concatenate([ref[:, c] for c in cols], axis=1) for ref in rows], axis=0)
        right = jnp.concatenate([part[...] for part in weights[n]], axis=0)
        term = jnp.dot(left, right, preferred_element_type=jnp.float32)
        total = term if total is None else total + term
    for i, out in enumerate(outs):
        out[0:FLAT, :] = total[i * FLAT : (i + 1) * FLAT].astype(jnp.bfloat16)


def wide_product_kernel(place, *refs):
    count = len(refs) - 10
    top, bottom, left_top, right_bottom, from_left, from_right = refs[count : count + 6]
    halves = lambda ref: (ref.at[0:512, :], ref.at[512:1024, :])
    left_bottom, far_top = halves(from_left)
    right_top, far_bottom = halves(from_right)
    weights = ((top, bottom), (left_top, left_bottom), (right_top, right_bottom), (far_top, far_bottom))
    multiply(place, refs[:count], weights, refs[count + 6 :])


def first_product_kernel(place, ints, *refs):
    buffers, outs, shards = refs[6:10], refs[10:14], refs[14]
    multiply(place, refs[:6], [(ref,) for ref in buffers], outs)
    owner, z = place[0], place[2]
    row = 0
    for piece in buffers:
        for t in range(piece.shape[0] // 32):
            shards[row : row + 8, :] = piece[t * 32 : t * 32 + 16, :].astype(jnp.float32)[:8]
            row += 8
    lane = lax.broadcasted_iota(jnp.int32, (8, 128), 1)

    def shard(device, shift):
        device = jnp.minimum(device, 127)
        turn = lax.rem(device // 16 % 4 + 4 - z, 4)
        at = jnp.where(turn == 0, 0, jnp.where(turn == 3, 1, turn + 1)) * 32
        at = (at + device // 64 * 16 + device % 16) * 8
        return pltpu.roll(shards[pl.ds(pl.multiple_of(at, 8), 8), :], lax.rem(shift, 128), 1)

    def unit(u, at):
        device = 4 * u // 5
        offset = 64 * u - 80 * device
        low = shard(device, at + 240 - offset)
        high = shard(device + 1, at + 192 - offset)
        return jnp.where(lane - at < 80 - offset, low, high)

    blocks = []
    for block in range(10):
        if block < 8:
            units = [ints[owner * OWN_HEADS + 2 * block + i] for i in range(2)]
        else:
            units = [HEADS + 16 * (block - 8) + 2 * ints[HEADS + owner] + i for i in range(2)]
        blocks.append(jnp.where(lane < 64, unit(units[0], 0), unit(units[1], 64)))
    taps = jnp.concatenate(blocks, axis=0).astype(jnp.bfloat16)
    for out in outs:
        out[FLAT : FLAT + 80, :] = taps


def silu(value):
    return value * jax.nn.sigmoid(value)


def convolve(inputs, stored, taps):
    window = [stored[j].astype(jnp.float32) for j in range(TAPS - 1)] + inputs
    outputs = []
    for moment in range(STEPS):
        total = taps[TAPS : TAPS + 1]
        for lag in range(TAPS):
            total = total + taps[lag : lag + 1] * window[moment + lag]
        outputs.append(silu(total).astype(jnp.bfloat16))
    return outputs


def gathered(place, pieces, buffer):
    quarter = 2 * place[1] + place[3]
    width = min(pieces[0].shape[1], 256)
    for i, piece in enumerate(pieces):
        for part in range(piece.shape[1] // width):
            at = pl.multiple_of(lax.bitwise_xor(quarter, i) * width + part * SPAN, 128)
            buffer[:, pl.ds(at, width)] = piece[:, part * width : (part + 1) * width]
    return [buffer[t * ROWS : (t + 1) * ROWS, :].astype(jnp.float32) for t in range(STEPS)]


def groups_kernel(place, *refs):
    pieces, (stored, out, dt, head_taps, buffer) = refs[:4], refs[4:]
    values = gathered(place, pieces, buffer)
    taps = buffer[FLAT : FLAT + 80, 384:512].astype(jnp.float32)
    for block in range(8):
        head_taps[:, block * 128 : (block + 1) * 128] = taps[block * 8 : block * 8 + 8]
    taps = jnp.concatenate([taps[64:72], taps[72:80]], axis=1)
    for t, value in enumerate(convolve([value[:, :256] for value in values], stored, taps)):
        out[t] = value
        dt[t] = values[t][:, 256:384].astype(jnp.bfloat16)


def state_kernel(state, every, c_all, mask, out, pair):
    chosen = mask[...]
    for r in range(8):
        read = lax.dot_general(
            c_all[r].astype(jnp.bfloat16),
            state[r].reshape(SPAN, STATE),
            (((1,), (1,)), ((), ())),
            preferred_element_type=jnp.float32,
        )
        for t in range(STEPS):
            rows = slice(8 * t, 8 * t + 8)
            out[t, r : r + 1, :] = jnp.sum(read[rows] * chosen, axis=0, keepdims=True)
    n = 0
    for t in range(STEPS):
        for s in range(t + 1):
            total = None
            for k in range(GROUPS):
                both = every[k, t, :, STATE:] * every[k, s, :, :STATE]
                term = jnp.sum(both, axis=1, keepdims=True) * mask[k : k + 1, :]
                total = term if total is None else total + term
            pair[n] = total
            n += 1


def scan_kernel(place, *refs):
    pieces, (stored, taps, *refs) = refs[:4], refs[4:]
    read, read_more, pair, pair_more, dt, spread, params, member, gated, squares, buffer = refs
    whole = lambda low, high, n: jnp.concatenate([low[n], high[n]], axis=0)
    both = gathered(place, pieces, buffer)
    inputs = [value[:, :SPAN] for value in both]
    values = [v.astype(jnp.float32) for v in convolve(inputs, stored, taps[...])]
    rate = params[0:1]
    bias = params[1:2]
    skip = params[2:3]
    keeps, driven = [], []
    for t in range(STEPS):
        raw = jnp.dot(dt[t], spread[...], preferred_element_type=jnp.float32)
        delta = jax.nn.softplus(raw + bias)
        keeps.append(jnp.exp(delta * rate))
        driven.append(delta * values[t])
    n = 0
    for t in range(STEPS):
        total = skip * values[t]
        offset = n + t
        after = None
        for s in range(t, -1, -1):
            term = whole(pair, pair_more, offset) * driven[s]
            total = total + (term if after is None else after * term)
            after = keeps[s] if after is None else after * keeps[s]
            offset -= 1
        value = (total + after * whole(read, read_more, t)) * silu(both[t][:, SPAN:])
        gated[t] = value * params[3:4]
        total = lax.dot_general(
            member[...], value * value, (((1,), (1,)), ((), ())), precision=HIGH, preferred_element_type=jnp.float32
        )
        total = jnp.concatenate([total, jnp.zeros((GROUPS, 128 - ROWS), jnp.float32)], axis=1)
        for to in range(8):
            squares[to, 8 * t : 8 * t + 8, :] = total
        n += t + 1


def norm_kernel(gated, squares, member, out):
    for t in range(STEPS):
        total = squares[0, 8 * t : 8 * t + 8, 0:ROWS]
        for owner in range(1, 8):
            total = total + squares[owner, 8 * t : 8 * t + 8, 0:ROWS]
        scale = lax.rsqrt(total / SPAN + norm_eps)
        lanes = lax.dot_general(
            scale, member[...], (((0,), (0,)), ((), ())), precision=HIGH, preferred_element_type=jnp.float32
        )
        out[t] = (gated[t] * lanes).astype(jnp.bfloat16)


def call(kernel, shapes, *args, scalars=0, scratch=(), limit=12):
    vmem = pl.BlockSpec(memory_space=pltpu.VMEM)
    smem = pl.BlockSpec(memory_space=pltpu.SMEM)
    return pl.pallas_call(
        kernel,
        in_specs=[smem] * scalars + [vmem] * (len(args) - scalars),
        out_specs=[vmem] * len(shapes),
        out_shape=[jax.ShapeDtypeStruct(s, d) for s, d in shapes],
        scratch_shapes=scratch,
        compiler_params=pltpu.CompilerParams(vmem_limit_bytes=limit * 2**20),
        name=kernel.__name__,
    )(*args)


def read_state(state, every, c_all, mask, first, count):
    return pl.pallas_call(
        state_kernel,
        grid=(count,),
        in_specs=[
            pl.BlockSpec((8, OWN_HEADS, HEAD_DIM, STATE), lambda i: (i + first, 0, 0, 0)),
            pl.BlockSpec((GROUPS, STEPS, 8, 2 * STATE), lambda i: (0, 0, i + first, 0)),
            pl.BlockSpec((8, 24, STATE), lambda i: (i + first, 0, 0)),
            pl.BlockSpec((8, SPAN), lambda i: (0, 0)),
        ],
        out_specs=[
            pl.BlockSpec((3, 8, SPAN), lambda i: (0, i, 0)),
            pl.BlockSpec((6, 8, SPAN), lambda i: (0, i, 0)),
        ],
        out_shape=[
            jax.ShapeDtypeStruct((3, 8 * count, SPAN), jnp.float32),
            jax.ShapeDtypeStruct((6, 8 * count, SPAN), jnp.float32),
        ],
        compiler_params=pltpu.CompilerParams(vmem_limit_bytes=50 * 2**20),
        name="read_state",
    )(state, every, c_all, mask)


def per_device(
    weight_master,
    weight_grad,
    weight_first,
    weight_second,
    conv_master,
    conv_grad,
    conv_first,
    conv_second,
    learn_rate,
    segment_offsets,
    head_order,
    group_order,
    hidden_input,
    scan_state,
    conv_heads,
    conv_groups,
    decay_log,
    delta_bias,
    skip_gain,
    norm_gain,
):
    owner = lax.axis_index("tp")
    side, z, core = lax.axis_index("x"), lax.axis_index("z"), lax.axis_index("c")
    up = lambda value: lax.ppermute(value, "z", [(i, (i + 1) % 4) for i in range(4)])
    down = lambda value: lax.ppermute(value, "z", [(i, (i + 3) % 4) for i in range(4)])

    def swap(value, turn):
        return lax.ppermute(value, ("x", "c"), [(i, i ^ turn) for i in range(4)])

    position = jnp.stack([owner, side, z, core]).astype(jnp.int32)
    ints = jnp.concatenate([head_order, group_order, segment_offsets])
    def after(value, *others):
        return lax.optimization_barrier((value, *others))[0]

    far = [swap(hidden_input[0], 2)]
    near = swap(hidden_input.reshape(FLAT, -1), 1)

    sent = refit(
        learn_rate, ints, head_order.reshape(1, HEADS),
        (conv_master, conv_grad, conv_first, conv_second),
        (weight_master, weight_grad, weight_first, weight_second),
    )
    owned = lax.all_to_all(after(sent, *far, near), ("x", "c", "tp"), split_axis=0, concat_axis=0, tiled=True)
    owned = owned.reshape(1024, 640)
    far.append(swap(after(hidden_input[1:].reshape(2 * ROWS, -1), owned), 2))

    def exchanged(outs):
        return [outs[0]] + [swap(outs[i], i) for i in range(1, 4)]

    row = lambda value: value.reshape(1, -1)
    params, member, mask, spread = call(
        tables_kernel,
        [
            ((8, SPAN), jnp.float32),
            ((GROUPS, SPAN), jnp.float32),
            ((GROUPS, SPAN), jnp.float32),
            ((128, SPAN), jnp.bfloat16),
        ],
        position, after(ints, sent), row(decay_log), row(delta_bias), row(skip_gain), row(norm_gain), scalars=2,
    )
    stored_heads = jnp.swapaxes(conv_heads, 0, 1)
    stored_groups = jnp.swapaxes(conv_groups.reshape(ROWS, TAPS - 1, 2 * STATE), 0, 1)

    own = owned[:, :128]
    halves = [owned[512 * i : 512 * i + 512, 128:] for i in range(2)]
    own_late, *halves = lax.optimization_barrier((own, *halves))
    pieces = [own, up(own_late), down(own), lax.ppermute(own, "z", [(i, (i + 2) % 4) for i in range(4)])]
    far_pair = after(far, *pieces[1:])
    rows = [hidden_input.reshape(FLAT, -1), near, *far, *[swap(value, 1) for value in far_pair]]
    top, bottom = [after(half, *pieces[1:]) for half in halves]
    left_top, right_bottom = up(top), down(bottom)

    first = call(
        first_product_kernel, [((FLAT + 80, 128), jnp.bfloat16)] * 4, position, ints, *rows, *pieces,
        scalars=2, scratch=[pltpu.VMEM((1024, 128), jnp.float32)], limit=20,
    )
    arrived = after((left_top, right_bottom), first)
    from_left = up(jnp.concatenate([bottom, arrived[0]]))
    from_right = down(jnp.concatenate([top, arrived[1]]))
    b_and_c, dt, head_taps = call(
        groups_kernel,
        [((STEPS, ROWS, 2 * STATE), jnp.bfloat16), ((STEPS, ROWS, 128), jnp.bfloat16), ((8, SPAN), jnp.float32)],
        position, *exchanged(first), stored_groups, scalars=1, scratch=[pltpu.VMEM((FLAT + 80, 512), jnp.bfloat16)],
    )
    ahead = lambda k: [(i, i // 4 * 4 + (i + 4 - k) % 4) for i in range(8)]
    every = jnp.stack([b_and_c] + [lax.ppermute(b_and_c, "tp", ahead(k)) for k in range(1, 4)])
    every = jnp.concatenate([every, lax.ppermute(every, "tp", [(i, i ^ 4) for i in range(8)])])
    every = every.astype(jnp.float32)
    c_all = every[..., STATE:].transpose(2, 1, 0, 3).reshape(ROWS, STEPS * GROUPS, STATE)
    read, pair = read_state(scan_state, every, c_all, mask, 0, 4)

    top, read = lax.optimization_barrier((top, read))
    second = call(
        wide_product_kernel, [((FLAT, 512), jnp.bfloat16)] * 4, position, *rows,
        top, bottom, left_top, right_bottom, from_left, from_right,
        scalars=1, limit=24,
    )
    c_all, *second = lax.optimization_barrier((c_all, *second))
    read_more, pair_more = read_state(scan_state, every, c_all, mask, 4, 2)
    second = exchanged(second)
    gated, squares = call(
        scan_kernel,
        [((STEPS, ROWS, SPAN), jnp.float32), ((8, STEPS * GROUPS, 128), jnp.float32)],
        position, *second, stored_heads, head_taps, read, read_more, pair, pair_more, dt, spread, params, member,
        scalars=1, scratch=[pltpu.VMEM((FLAT, 2 * SPAN), jnp.bfloat16)], limit=20,
    )
    squares = lax.all_to_all(squares, "tp", split_axis=0, concat_axis=0, tiled=True)
    (mixer_out,) = call(
        norm_kernel, [((STEPS, ROWS, SPAN), jnp.bfloat16)], gated, squares, member
    )
    return mixer_out


def solution(mesh):
    mesh = Mesh(mesh.devices.reshape(2, 4, 2, 8), ("x", "z", "c", "tp"))
    fsdp = ("x", "z", "c")
    every = fsdp + ("tp",)
    return jax.shard_map(
        per_device,
        mesh=mesh,
        in_specs=(P(every, None),) * 4
        + (P(None, every),) * 4
        + (P(),) * 4
        + (P(None, fsdp, None), P(fsdp, "tp", None, None), P(fsdp, None, "tp"), P(fsdp, None, None, "tp", None))
        + (P(),) * 4,
        out_specs=P(None, fsdp, "tp"),
        check_vma=False,
    )
```

```python
import functools

import jax
import jax.numpy as jnp
from jax import lax
from jax.experimental import pallas as pl
from jax.experimental.pallas import tpu as pltpu
from jax.sharding import Mesh
from jax.sharding import PartitionSpec as P

TAPS = 4
ADAM_STEP = 100
STEPS = 3
ROWS = 48
FLAT = STEPS * ROWS
HEADS = 128
GROUPS = 8
HEAD_DIM = 64
STATE = 128
OWN_HEADS = 16
SPAN = OWN_HEADS * HEAD_DIM
JOINED = 18560
PIECE = 640
PIECES = JOINED // PIECE
SHARD = 80
INNER = HEADS * HEAD_DIM

beta_one = 0.9
beta_two = 0.95
adam_eps = 1e-08
weight_decay = 0.1
norm_eps = 1e-05
HIGH = lax.Precision.HIGHEST


def adamw(master, gradient, first, second, rate):
    slope = gradient.astype(jnp.float32)
    moment_one = beta_one * first + (1.0 - beta_one) * slope
    moment_two = beta_two * second + (1.0 - beta_two) * slope * slope
    fixed_one = moment_one / (1.0 - beta_one**ADAM_STEP)
    fixed_two = moment_two / (1.0 - beta_two**ADAM_STEP)
    update = fixed_one / (jnp.sqrt(fixed_two) + adam_eps) + weight_decay * master
    return (master - rate * update).astype(jnp.bfloat16)


def refit_kernel(
    ints, order, rate, conv_m, conv_g, conv_f, conv_s, master, grad, first, second,
    out, work, m, g, f, s, sems,
):
    copies = []
    for p in range(PIECES):
        cols = pl.ds(p * PIECE, PIECE)
        copies.append(
            [
                pltpu.make_async_copy(hbm.at[:, cols], vmem.at[:, cols], sems.at[p, i])
                for i, (hbm, vmem) in enumerate(((master, m), (grad, g), (first, f), (second, s)))
            ]
        )
    for piece in copies:
        for copy in piece:
            copy.start()
    for p, piece in enumerate(copies):
        for copy in piece:
            copy.wait()
        for j in range(p * PIECE, (p + 1) * PIECE, 128):
            cols = slice(j, j + 128)
            work[:, cols] = adamw(m[:, cols], g[:, cols], f[:, cols], s[:, cols], rate[...]).astype(jnp.float32)

    lane = lax.broadcasted_iota(jnp.int32, (32, 128), 1)
    conv = adamw(conv_m[...], conv_g[...], conv_f[...], conv_s[...], rate[...])
    shift = lax.broadcasted_iota(jnp.int32, (SHARD, 128), 1) - lax.broadcasted_iota(jnp.int32, (SHARD, 128), 0) == 16
    conv = jnp.dot(conv, shift.astype(jnp.bfloat16), preferred_element_type=jnp.float32)
    conv = jnp.concatenate([conv, jnp.zeros((27, 128), jnp.float32)], axis=0)
    offsets = [ints[HEADS + GROUPS + i] for i in range(5)]
    dt = work[:, pl.ds(pl.multiple_of(offsets[4], 128), 128)]
    onehot = (lax.broadcasted_iota(jnp.int32, (HEADS, HEADS), 0) == order[...]).astype(jnp.bfloat16)
    dt = jnp.dot(dt.astype(jnp.bfloat16), onehot, preferred_element_type=jnp.float32)

    def block(start):
        return work[:, pl.ds(pl.multiple_of(start, 128), 128)]

    def half(start, head, low):
        wide = block(start + (head // 2) * 128)
        turn = (head % 2) != (0 if low else 1)
        return jnp.where(turn, pltpu.roll(wide, 64, 1), wide)

    for owner in range(8):
        group = ints[HEADS + owner]
        mine = dt if owner == 0 else pltpu.roll(dt, 128 - 16 * owner, 1)
        leading = (block(offsets[2] + group * 128), block(offsets[3] + group * 128), jnp.where(lane < 16, mine, 0.0), conv)
        for quarter in range(4):
            to = quarter * 8 + owner
            out[to, :, 0:128] = leading[quarter].astype(jnp.bfloat16)
            for k in range(2):
                low = ints[owner * OWN_HEADS + 4 * quarter + 2 * k]
                high = ints[owner * OWN_HEADS + 4 * quarter + 2 * k + 1]
                for segment, at in ((1, 128), (0, 384)):
                    start = offsets[segment]
                    both = jnp.where(lane < 64, half(start, low, True), half(start, high, False))
                    out[to, :, at + k * 128 : at + (k + 1) * 128] = both.astype(jnp.bfloat16)


def refit(rate, ints, order, conv, weight):
    vmem = pl.BlockSpec(memory_space=pltpu.VMEM)
    hbm = pl.BlockSpec(memory_space=pltpu.HBM)
    return pl.pallas_call(
        refit_kernel,
        in_specs=[pl.BlockSpec(memory_space=pltpu.SMEM)] + [vmem] * 6 + [hbm] * 4,
        out_specs=vmem,
        out_shape=jax.ShapeDtypeStruct((32, 32, 640), jnp.bfloat16),
        scratch_shapes=[
            pltpu.VMEM((32, JOINED), jnp.float32),
            pltpu.VMEM((32, JOINED), jnp.float32),
            pltpu.VMEM((32, JOINED), jnp.bfloat16),
            pltpu.VMEM((32, JOINED), jnp.float32),
            pltpu.VMEM((32, JOINED), jnp.float32),
            pltpu.SemaphoreType.DMA((PIECES, 4)),
        ],
        compiler_params=pltpu.CompilerParams(vmem_limit_bytes=58 * 2**20),
        name="refit",
    )(ints, order, rate.reshape(1, 1), *conv, *weight)


def tables_kernel(place, ints, decay, bias, skip, gain, lanes, member, mask, spread):
    owner = place[0]
    lane = lax.broadcasted_iota(jnp.int32, (1, 128), 1)
    heads = []
    for k in range(8):
        low = ints[owner * OWN_HEADS + 2 * k]
        high = ints[owner * OWN_HEADS + 2 * k + 1]
        heads.append(jnp.where(lane < 64, low, high))
        halves = []
        for head, odd in ((low, 0), (high, 1)):
            wide = gain[:, pl.ds(pl.multiple_of(head // 2 * 128, 128), 128)]
            halves.append(jnp.where(head % 2 != odd, pltpu.roll(wide, 64, 1), wide))
        lanes[3:4, k * 128 : (k + 1) * 128] = jnp.where(lane < 64, halves[0], halves[1])
    heads = jnp.concatenate(heads, axis=1)
    onehot = (lax.broadcasted_iota(jnp.int32, (HEADS, SPAN), 0) == heads).astype(jnp.float32)
    rows = jnp.concatenate([-jnp.exp(decay[...]), bias[...], skip[...], jnp.zeros((5, HEADS), jnp.float32)], axis=0)
    lanes[0:3, :] = jnp.dot(rows, onehot, precision=HIGH, preferred_element_type=jnp.float32)[0:3]
    group = heads // OWN_HEADS
    member[...] = (lax.broadcasted_iota(jnp.int32, (GROUPS, SPAN), 0) == group).astype(jnp.float32)
    for k in range(GROUPS):
        partner = lax.rem(owner // 4 * 4 + k // 4 * 4, 8) + lax.rem(owner + k, 4)
        mask[k : k + 1, :] = (group == ints[HEADS + partner]).astype(jnp.float32)
    slot = lax.broadcasted_iota(jnp.int32, (128, SPAN), 1) // HEAD_DIM
    spread[...] = (lax.broadcasted_iota(jnp.int32, (128, SPAN), 0) == slot).astype(jnp.bfloat16)


def multiply(place, rows, weights, outs):
    total = None
    for n, turn in enumerate((0, 3, 1, 2)):
        at = lax.rem(place[2] + turn, 4)
        cols = [pl.ds(pl.multiple_of((x * 4 + at) * 512, 512), 512) for x in range(2)]
        left = jnp.concatenate([jnp.concatenate([ref[:, c] for c in cols], axis=1) for ref in rows], axis=0)
        right = jnp.concatenate([part[...] for part in weights[n]], axis=0)
        term = jnp.dot(left, right, preferred_element_type=jnp.float32)
        total = term if total is None else total + term
    for i, out in enumerate(outs):
        out[0:FLAT, :] = total[i * FLAT : (i + 1) * FLAT].astype(jnp.bfloat16)


def wide_product_kernel(place, *refs):
    count = len(refs) - 10
    top, bottom, left_top, right_bottom, from_left, from_right = refs[count : count + 6]
    halves = lambda ref: (ref.at[0:512, :], ref.at[512:1024, :])
    left_bottom, far_top = halves(from_left)
    right_top, far_bottom = halves(from_right)
    weights = ((top, bottom), (left_top, left_bottom), (right_top, right_bottom), (far_top, far_bottom))
    multiply(place, refs[:count], weights, refs[count + 6 :])


def first_product_kernel(place, ints, *refs):
    buffers, outs, shards = refs[6:10], refs[10:14], refs[14]
    multiply(place, refs[:6], [(ref,) for ref in buffers], outs)
    owner, z = place[0], place[2]
    row = 0
    for piece in buffers:
        for t in range(piece.shape[0] // 32):
            shards[row : row + 8, :] = piece[t * 32 : t * 32 + 16, :].astype(jnp.float32)[:8]
            row += 8
    lane = lax.broadcasted_iota(jnp.int32, (8, 128), 1)

    def shard(device, shift):
        device = jnp.minimum(device, 127)
        turn = lax.rem(device // 16 % 4 + 4 - z, 4)
        at = jnp.where(turn == 0, 0, jnp.where(turn == 3, 1, turn + 1)) * 32
        at = (at + device // 64 * 16 + device % 16) * 8
        return pltpu.roll(shards[pl.ds(pl.multiple_of(at, 8), 8), :], lax.rem(shift, 128), 1)

    def unit(u, at):
        device = 4 * u // 5
        offset = 64 * u - 80 * device
        low = shard(device, at + 240 - offset)
        high = shard(device + 1, at + 192 - offset)
        return jnp.where(lane - at < 80 - offset, low, high)

    blocks = []
    for block in range(10):
        if block < 8:
            units = [ints[owner * OWN_HEADS + 2 * block + i] for i in range(2)]
        else:
            units = [HEADS + 16 * (block - 8) + 2 * ints[HEADS + owner] + i for i in range(2)]
        blocks.append(jnp.where(lane < 64, unit(units[0], 0), unit(units[1], 64)))
    taps = jnp.concatenate(blocks, axis=0).astype(jnp.bfloat16)
    for out in outs:
        out[FLAT : FLAT + 80, :] = taps


def silu(value):
    return value * jax.nn.sigmoid(value)


def convolve(inputs, stored, taps):
    window = [stored[j].astype(jnp.float32) for j in range(TAPS - 1)] + inputs
    outputs = []
    for moment in range(STEPS):
        total = taps[TAPS : TAPS + 1]
        for lag in range(TAPS):
            total = total + taps[lag : lag + 1] * window[moment + lag]
        outputs.append(silu(total).astype(jnp.bfloat16))
    return outputs


def gathered(place, pieces, buffer):
    quarter = 2 * place[1] + place[3]
    width = min(pieces[0].shape[1], 256)
    for i, piece in enumerate(pieces):
        for part in range(piece.shape[1] // width):
            at = pl.multiple_of(lax.bitwise_xor(quarter, i) * width + part * SPAN, 128)
            buffer[:, pl.ds(at, width)] = piece[:, part * width : (part + 1) * width]
    return [buffer[t * ROWS : (t + 1) * ROWS, :].astype(jnp.float32) for t in range(STEPS)]


def groups_kernel(place, *refs):
    pieces, (stored, out, dt, head_taps, buffer) = refs[:4], refs[4:]
    values = gathered(place, pieces, buffer)
    taps = buffer[FLAT : FLAT + 80, 384:512].astype(jnp.float32)
    for block in range(8):
        head_taps[:, block * 128 : (block + 1) * 128] = taps[block * 8 : block * 8 + 8]
    taps = jnp.concatenate([taps[64:72], taps[72:80]], axis=1)
    for t, value in enumerate(convolve([value[:, :256] for value in values], stored, taps)):
        out[t] = value
        dt[t] = values[t][:, 256:384].astype(jnp.bfloat16)


def state_kernel(state, every, c_all, mask, out, pair):
    chosen = mask[...]
    for r in range(8):
        read = lax.dot_general(
            c_all[r].astype(jnp.bfloat16),
            state[r].reshape(SPAN, STATE),
            (((1,), (1,)), ((), ())),
            preferred_element_type=jnp.float32,
        )
        for t in range(STEPS):
            rows = slice(8 * t, 8 * t + 8)
            out[t, r : r + 1, :] = jnp.sum(read[rows] * chosen, axis=0, keepdims=True)
    n = 0
    for t in range(STEPS):
        for s in range(t + 1):
            total = None
            for k in range(GROUPS):
                both = every[k, t, :, STATE:] * every[k, s, :, :STATE]
                term = jnp.sum(both, axis=1, keepdims=True) * mask[k : k + 1, :]
                total = term if total is None else total + term
            pair[n] = total
            n += 1


def scan_kernel(place, *refs):
    pieces, (stored, taps, *refs) = refs[:4], refs[4:]
    read, read_more, pair, pair_more, dt, spread, params, member, gated, squares, buffer = refs
    whole = lambda low, high, n: jnp.concatenate([low[n], high[n]], axis=0)
    both = gathered(place, pieces, buffer)
    inputs = [value[:, :SPAN] for value in both]
    values = [v.astype(jnp.float32) for v in convolve(inputs, stored, taps[...])]
    rate = params[0:1]
    bias = params[1:2]
    skip = params[2:3]
    keeps, driven = [], []
    for t in range(STEPS):
        raw = jnp.dot(dt[t], spread[...], preferred_element_type=jnp.float32)
        delta = jax.nn.softplus(raw + bias)
        keeps.append(jnp.exp(delta * rate))
        driven.append(delta * values[t])
    n = 0
    for t in range(STEPS):
        total = skip * values[t]
        offset = n + t
        after = None
        for s in range(t, -1, -1):
            term = whole(pair, pair_more, offset) * driven[s]
            total = total + (term if after is None else after * term)
            after = keeps[s] if after is None else after * keeps[s]
            offset -= 1
        value = (total + after * whole(read, read_more, t)) * silu(both[t][:, SPAN:])
        gated[t] = value * params[3:4]
        total = lax.dot_general(
            member[...], value * value, (((1,), (1,)), ((), ())), precision=HIGH, preferred_element_type=jnp.float32
        )
        total = jnp.concatenate([total, jnp.zeros((GROUPS, 128 - ROWS), jnp.float32)], axis=1)
        for to in range(8):
            squares[to, 8 * t : 8 * t + 8, :] = total
        n += t + 1


def norm_kernel(gated, squares, member, out):
    for t in range(STEPS):
        total = squares[0, 8 * t : 8 * t + 8, 0:ROWS]
        for owner in range(1, 8):
            total = total + squares[owner, 8 * t : 8 * t + 8, 0:ROWS]
        scale = lax.rsqrt(total / SPAN + norm_eps)
        lanes = lax.dot_general(
            scale, member[...], (((0,), (0,)), ((), ())), precision=HIGH, preferred_element_type=jnp.float32
        )
        out[t] = (gated[t] * lanes).astype(jnp.bfloat16)


def call(kernel, shapes, *args, scalars=0, scratch=(), limit=12):
    vmem = pl.BlockSpec(memory_space=pltpu.VMEM)
    smem = pl.BlockSpec(memory_space=pltpu.SMEM)
    return pl.pallas_call(
        kernel,
        in_specs=[smem] * scalars + [vmem] * (len(args) - scalars),
        out_specs=[vmem] * len(shapes),
        out_shape=[jax.ShapeDtypeStruct(s, d) for s, d in shapes],
        scratch_shapes=scratch,
        compiler_params=pltpu.CompilerParams(vmem_limit_bytes=limit * 2**20),
        name=kernel.__name__,
    )(*args)


def read_state(state, every, c_all, mask, first, count):
    return pl.pallas_call(
        state_kernel,
        grid=(count,),
        in_specs=[
            pl.BlockSpec((8, OWN_HEADS, HEAD_DIM, STATE), lambda i: (i + first, 0, 0, 0)),
            pl.BlockSpec((GROUPS, STEPS, 8, 2 * STATE), lambda i: (0, 0, i + first, 0)),
            pl.BlockSpec((8, 24, STATE), lambda i: (i + first, 0, 0)),
            pl.BlockSpec((8, SPAN), lambda i: (0, 0)),
        ],
        out_specs=[
            pl.BlockSpec((3, 8, SPAN), lambda i: (0, i, 0)),
            pl.BlockSpec((6, 8, SPAN), lambda i: (0, i, 0)),
        ],
        out_shape=[
            jax.ShapeDtypeStruct((3, 8 * count, SPAN), jnp.float32),
            jax.ShapeDtypeStruct((6, 8 * count, SPAN), jnp.float32),
        ],
        compiler_params=pltpu.CompilerParams(vmem_limit_bytes=50 * 2**20),
        name="read_state",
    )(state, every, c_all, mask)


def per_device(
    weight_master,
    weight_grad,
    weight_first,
    weight_second,
    conv_master,
    conv_grad,
    conv_first,
    conv_second,
    learn_rate,
    segment_offsets,
    head_order,
    group_order,
    hidden_input,
    scan_state,
    conv_heads,
    conv_groups,
    decay_log,
    delta_bias,
    skip_gain,
    norm_gain,
):
    owner = lax.axis_index("tp")
    side, z, core = lax.axis_index("x"), lax.axis_index("z"), lax.axis_index("c")
    up = lambda value: lax.ppermute(value, "z", [(i, (i + 1) % 4) for i in range(4)])
    down = lambda value: lax.ppermute(value, "z", [(i, (i + 3) % 4) for i in range(4)])

    def swap(value, turn):
        return lax.ppermute(value, ("x", "c"), [(i, i ^ turn) for i in range(4)])

    position = jnp.stack([owner, side, z, core]).astype(jnp.int32)
    ints = jnp.concatenate([head_order, group_order, segment_offsets])
    def after(value, *others):
        return lax.optimization_barrier((value, *others))[0]

    far = [swap(hidden_input[0], 2)]
    near = swap(hidden_input.reshape(FLAT, -1), 1)

    sent = refit(
        learn_rate, ints, head_order.reshape(1, HEADS),
        (conv_master, conv_grad, conv_first, conv_second),
        (weight_master, weight_grad, weight_first, weight_second),
    )
    owned = lax.all_to_all(after(sent, *far, near), ("x", "c", "tp"), split_axis=0, concat_axis=0, tiled=True)
    owned = owned.reshape(1024, 640)
    far.append(swap(after(hidden_input[1:].reshape(2 * ROWS, -1), owned), 2))

    def exchanged(outs):
        return [outs[0]] + [swap(outs[i], i) for i in range(1, 4)]

    row = lambda value: value.reshape(1, -1)
    params, member, mask, spread = call(
        tables_kernel,
        [
            ((8, SPAN), jnp.float32),
            ((GROUPS, SPAN), jnp.float32),
            ((GROUPS, SPAN), jnp.float32),
            ((128, SPAN), jnp.bfloat16),
        ],
        position, after(ints, sent), row(decay_log), row(delta_bias), row(skip_gain), row(norm_gain), scalars=2,
    )
    stored_heads = jnp.swapaxes(conv_heads, 0, 1)
    stored_groups = jnp.swapaxes(conv_groups.reshape(ROWS, TAPS - 1, 2 * STATE), 0, 1)

    own = owned[:, :128]
    halves = [owned[512 * i : 512 * i + 512, 128:] for i in range(2)]
    own_late, *halves = lax.optimization_barrier((own, *halves))
    pieces = [own, up(own_late), down(own), lax.ppermute(own, "z", [(i, (i + 2) % 4) for i in range(4)])]
    far_pair = after(far, *pieces[1:])
    rows = [hidden_input.reshape(FLAT, -1), near, *far, *[swap(value, 1) for value in far_pair]]
    top, bottom = [after(half, *pieces[1:]) for half in halves]
    left_top, right_bottom = up(top), down(bottom)

    first = call(
        first_product_kernel, [((FLAT + 80, 128), jnp.bfloat16)] * 4, position, ints, *rows, *pieces,
        scalars=2, scratch=[pltpu.VMEM((1024, 128), jnp.float32)], limit=20,
    )
    arrived = after((left_top, right_bottom), first)
    from_left = up(jnp.concatenate([bottom, arrived[0]]))
    from_right = down(jnp.concatenate([top, arrived[1]]))
    b_and_c, dt, head_taps = call(
        groups_kernel,
        [((STEPS, ROWS, 2 * STATE), jnp.bfloat16), ((STEPS, ROWS, 128), jnp.bfloat16), ((8, SPAN), jnp.float32)],
        position, *exchanged(first), stored_groups, scalars=1, scratch=[pltpu.VMEM((FLAT + 80, 512), jnp.bfloat16)],
    )
    ahead = lambda k: [(i, i // 4 * 4 + (i + 4 - k) % 4) for i in range(8)]
    every = jnp.stack([b_and_c] + [lax.ppermute(b_and_c, "tp", ahead(k)) for k in range(1, 4)])
    every = jnp.concatenate([every, lax.ppermute(every, "tp", [(i, i ^ 4) for i in range(8)])])
    every = every.astype(jnp.float32)
    c_all = every[..., STATE:].transpose(2, 1, 0, 3).reshape(ROWS, STEPS * GROUPS, STATE)
    read, pair = read_state(scan_state, every, c_all, mask, 0, 4)

    top, read = lax.optimization_barrier((top, read))
    second = call(
        wide_product_kernel, [((FLAT, 512), jnp.bfloat16)] * 4, position, *rows,
        top, bottom, left_top, right_bottom, from_left, from_right,
        scalars=1, limit=24,
    )
    c_all, *second = lax.optimization_barrier((c_all, *second))
    read_more, pair_more = read_state(scan_state, every, c_all, mask, 4, 2)
    second = exchanged(second)
    gated, squares = call(
        scan_kernel,
        [((STEPS, ROWS, SPAN), jnp.float32), ((8, STEPS * GROUPS, 128), jnp.float32)],
        position, *second, stored_heads, head_taps, read, read_more, pair, pair_more, dt, spread, params, member,
        scalars=1, scratch=[pltpu.VMEM((FLAT, 2 * SPAN), jnp.bfloat16)], limit=20,
    )
    squares = lax.all_to_all(squares, "tp", split_axis=0, concat_axis=0, tiled=True)
    (mixer_out,) = call(
        norm_kernel, [((STEPS, ROWS, SPAN), jnp.bfloat16)], gated, squares, member
    )
    return mixer_out


def solution(mesh):
    mesh = Mesh(mesh.devices.reshape(2, 4, 2, 8), ("x", "z", "c", "tp"))
    fsdp = ("x", "z", "c")
    every = fsdp + ("tp",)
    return jax.shard_map(
        per_device,
        mesh=mesh,
        in_specs=(P(every, None),) * 4
        + (P(None, every),) * 4
        + (P(),) * 4
        + (P(None, fsdp, None), P(fsdp, "tp", None, None), P(fsdp, None, "tp"), P(fsdp, None, None, "tp", None))
        + (P(),) * 4,
        out_specs=P(None, fsdp, "tp"),
        check_vma=False,
    )
```
